256 devices in a mesh: batch: 8 (over y, core), expert: 32 (over z, x).
Axes of the slice: x: 4, y: 4, z: 8, core: 2. Of those that a mesh axis runs over, the one named last changes fastest.
Arguments:
- layer_in: bfloat16 [2, 32, 64, 2048], P(None, 'expert', 'batch'), may hold values from -6 to 6
- queries: bfloat16 [2, 32, 64, 2048], P(None, 'expert', 'batch'), may hold values from -6 to 6
- fresh_entries: bfloat16 [2, 32, 64, 4096], P(None, 'expert', 'batch'), may hold values from -6 to 6
- cross_queries: bfloat16 [2, 32, 64, 2048], P(None, 'expert', 'batch'), may hold values from -6 to 6
- past_cache: bfloat16 [32, 64, 14, 4096], P('expert', 'batch'), may hold values from -5 to 5
- encoder_states: bfloat16 [32, 16, 32, 4096], P('expert', 'batch'), may hold values from -5 to 5
- source_lengths: int32 [32, 16], P('expert', 'batch'), may hold values from 2 to 32, as said below
- parents: int32 [2, 32, 64], P(None, 'expert'), may hold values from 0 to 63, as said below
- expert_ids: int32 [2, 32, 64, 2], P(None, 'expert'), may hold values from 0 to 63, all different within a row; in each aligned block of 64 rows (0 to 63, 64 to 127, ..., all dimensions but the last counted through in order) at most 4 rows name the same one
- gate_weights: float32 [2, 32, 64, 2], P(None, 'expert'), may hold values from 0.2 to 1
- norm_gain: bfloat16 [2048], replicated, may hold values from 0.25 to 1.75
- up_weight: bfloat16 [64, 2048, 4096], P('expert', None, 'batch'), may hold values from -0.125 to 0.125
- down_weight: bfloat16 [64, 4096, 2048], P('expert', 'batch'), may hold values from -0.09375 to 0.09375
Outputs:
- layer_out: bfloat16 [2, 32, 64, 2048], P(None, 'expert', 'batch')
- cache_out: bfloat16 [32, 64, 16, 4096], P('expert', 'batch')
The draws below stay inside these ranges and needn't reach their ends.
Inputs may be any that keep to these rules, and one draw needn't show every extreme that they name: For each step and group, parents is a permutation of the group's 64 rows, numbered within the group; rows with equal r // 8 are one device's slots. The slots of one device take exactly 2 rows held by other devices, at most one from each, and give exactly 2 of their rows to other devices, at most one to each. `expert_ids`: each row names two different experts. Within one step and one group no expert is named by more than 4 rows. `source_lengths`: in every group some sentence has all 32 positions.
All inputs are finite; a program needn't handle non-finite values.
Results may differ from the reference program's by a relative error of at most 0.0044.
Values may be sent and summed in bfloat16 or wider, within the bound.
A program may use at most 64 MiB of HBM per device.

```python
import math
import jax
import jax.numpy as jnp
import numpy as np
from jax import lax

D = 2048
HEADS = 16
DH = 128
HID = 4096
EXPERTS = 64
SLOTS = 8
BEAM = 4
GROUP_ROWS = 64
GROUPS = 32
CACHE = 14
SRC = 32
CAP = 4
MOVE = 2
STEPS = 2


def draw_queries(key, part):
    key = jax.random.fold_in(key, 11)
    shape = (STEPS, GROUPS, GROUP_ROWS, D)
    values = jnp.clip(jax.random.normal(key, shape, jnp.float32), -5.0, 5.0)
    return values.astype(jnp.bfloat16)


def draw_cross_queries(key, part):
    key = jax.random.fold_in(key, 13)
    shape = (STEPS, GROUPS, GROUP_ROWS, D)
    values = jnp.clip(jax.random.normal(key, shape, jnp.float32), -5.0, 5.0)
    return values.astype(jnp.bfloat16)


def draw_past_cache(key, part):
    key = jax.random.fold_in(key, 17)
    shape = (GROUPS, GROUP_ROWS, CACHE, 2 * D)
    values = jnp.clip(jax.random.normal(key, shape, jnp.float32), -5.0, 5.0)
    return values.astype(jnp.bfloat16)


def draw_encoder_states(key, part):
    key = jax.random.fold_in(key, 19)
    shape = (GROUPS, GROUP_ROWS // BEAM, SRC, 2 * D)
    values = jnp.clip(jax.random.normal(key, shape, jnp.float32), -5.0, 5.0)
    return values.astype(jnp.bfloat16)


def draw_source_lengths(key, part):
    key = jax.random.fold_in(key, 23)
    length_key, full_key = jax.random.split(key)
    sentences = GROUP_ROWS // BEAM
    lengths = jax.random.randint(length_key, (GROUPS, sentences), 2, SRC + 1)
    full_place = jax.random.randint(full_key, (GROUPS, 1), 0, sentences)
    return jnp.where(jnp.arange(sentences)[None, :] == full_place, SRC, lengths).astype(jnp.int32)


def group_order(key):
    devices = GROUP_ROWS // SLOTS
    offset_key, source_key, target_key = jax.random.split(key, 3)
    offsets = jax.random.permutation(offset_key, devices - 1) + 1
    source_perm = jax.vmap(lambda subkey: jax.random.permutation(subkey, SLOTS))(jax.random.split(source_key, devices))
    target_perm = jax.vmap(lambda subkey: jax.random.permutation(subkey, SLOTS))(jax.random.split(target_key, devices))
    device_ids = jnp.arange(devices)[:, None]
    slot_ids = jnp.arange(SLOTS)[None, :]
    shift = jnp.where(slot_ids < MOVE, offsets[jnp.minimum(slot_ids, MOVE - 1)], 0)
    source_dev = (device_ids + shift) % devices
    source_row = source_perm[source_dev, jnp.broadcast_to(slot_ids, source_dev.shape)]
    target = (device_ids * SLOTS + target_perm).reshape(-1)
    values = (source_dev * SLOTS + source_row).reshape(-1).astype(jnp.int32)
    return jnp.zeros((GROUP_ROWS,), jnp.int32).at[target].set(values)


def draw_parents(key, part):
    key = jax.random.fold_in(key, 29)
    orders = jax.vmap(group_order)(jax.random.split(key, STEPS * GROUPS))
    return orders.reshape(STEPS, GROUPS, GROUP_ROWS).astype(jnp.int32)


def block_scale(rng, extent, cuts, least, high):
    gain = 1.0
    for dim, shards_of in cuts:
        draws = jax.random.uniform(jax.random.fold_in(jax.random.fold_in(rng, 6), dim), (shards_of,), jnp.float32, least / len(cuts), high / len(cuts))
        gain = gain * jnp.repeat(jnp.exp(draws), extent[dim] // shards_of).reshape((-1,) + (1,) * (len(extent) - 1 - dim))
    return gain


def deal_out(key, own, number, rows, amount, top, reach, slope):
    ranking = jax.random.permutation(key, amount)
    heavy_load, common = load_shares(amount, rows * top, reach, slope, True), load_shares(amount, rows * top, reach, slope, False)
    places = jnp.arange(amount)

    def named(tallies, rotation):
        used = int((tallies > 0).sum())
        fixed = max(1, used // 4)
        moved = fixed + (places - fixed + rotation * (used - fixed)) % max(1, amount - fixed)
        return jnp.zeros((amount,), jnp.int32).at[ranking[jnp.where(places < fixed, places, moved)]].set(jnp.asarray(tallies, jnp.int32))

    tallies = jnp.where(number % 4 == 0, named(heavy_load, number // 4), named(common, number - number // 4 - 1))
    mixed = jax.random.permutation(jax.random.fold_in(own, 3), amount)
    giver, taker = mixed[0:amount // 2 * 2:2], mixed[1:amount // 2 * 2:2]
    margin = jnp.minimum(tallies[giver] - 1, reach - tallies[taker]) // 2
    margin = jnp.where((giver == ranking[0]) | (taker == ranking[0]) | (tallies[taker] == 0), 0, jnp.maximum(margin, 0))
    moved = jax.random.randint(jax.random.fold_in(own, 4), (amount // 2,), 0, 1 << 20) % (margin + 1)
    tallies = tallies.at[giver].add(-moved).at[taker].add(moved)
    members = jnp.searchsorted(jnp.cumsum(tallies), jnp.arange(rows * top), side="right").astype(jnp.int32)
    table = members.reshape(top, rows).T
    table = table[jax.random.permutation(jax.random.fold_in(own, 1), rows)]
    rotation = jax.random.randint(jax.random.fold_in(own, 2), (rows, 1), 0, top)
    return jnp.take_along_axis(table, (jnp.arange(top)[None, :] + rotation) % top, axis=1)


def load_shares(amount, total, limit, skew, full):
    portions = [(1 << 20) // math.isqrt(grade ** skew) + 1 for grade in range(1, amount + 1)]
    largest = limit if full else min(limit, max(-(-total // amount), total * portions[0] // sum(portions)))
    least = 1 if total - largest >= amount - 1 else 0
    given, rest = [largest] + [least] * (amount - 1), total - largest - least * (amount - 1)
    while rest > 0:
        candidates = [i for i in range(1, amount) if given[i] < largest] or [i for i in range(1, amount) if given[i] < limit]
        whole, remaining = sum([portions[i] for i in candidates]), rest
        for i in candidates:
            extra = min(limit - given[i], max(1, remaining * portions[i] // whole), rest)
            given[i] = given[i] + extra
            rest = rest - extra
    return np.array(given)


def scatter_about(own_key, dims, deviation, reach, cuts=(), kind=jnp.bfloat16):
    gain = block_scale(own_key, dims, cuts, -0.22, 0.18) if cuts else 1.0
    drawn = jax.random.normal(own_key, dims, jnp.float32) * deviation * gain
    return jnp.minimum(jnp.maximum(drawn, -reach), reach).astype(kind)


def setup_inputs(seed: int = 0) -> dict:
    seeds = jax.random.split(jax.random.key(seed), 14)
    layer_in = scatter_about(seeds[0], (STEPS, GROUPS, GROUP_ROWS, D), 1.0, 6.0, ((1, 32), (2, 8)))
    queries = draw_queries(jax.random.fold_in(seeds[13], 71), 0)
    fresh_entries = scatter_about(seeds[2], (STEPS, GROUPS, GROUP_ROWS, 2 * D), 1.0, 6.0, ((1, 32), (2, 8)))
    cross_queries = draw_cross_queries(jax.random.fold_in(seeds[13], 71), 0)
    past_cache = draw_past_cache(jax.random.fold_in(seeds[13], 71), 0)
    encoder_states = draw_encoder_states(jax.random.fold_in(seeds[13], 71), 0)
    source_lengths = draw_source_lengths(jax.random.fold_in(seeds[13], 71), 0)
    parents = draw_parents(jax.random.fold_in(seeds[13], 71), 0)
    expert_ids_keys = jax.random.split(jax.random.fold_in(seeds[8], 1), STEPS * GROUPS * GROUP_ROWS // GROUP_ROWS)
    expert_ids_turns = jax.random.permutation(jax.random.fold_in(seeds[8], 3), STEPS * GROUPS * GROUP_ROWS // GROUP_ROWS)
    expert_ids = jax.vmap(lambda own, number: deal_out(jax.random.fold_in(seeds[8], 2), own, number, GROUP_ROWS, EXPERTS, 2, CAP, 2))(expert_ids_keys, expert_ids_turns).reshape((STEPS, GROUPS, GROUP_ROWS, 2))
    gate_weights = jnp.clip(0.2 + 0.8 * jax.random.uniform(seeds[9], (STEPS, GROUPS, GROUP_ROWS, 2), jnp.float32) ** block_scale(seeds[9], (STEPS, GROUPS, GROUP_ROWS, 2), ((1, 32),), -0.2, 0.2), 0.2, 1.0)
    norm_gain = jnp.clip(1.0 + 0.15 * jax.random.normal(seeds[10], (D,), jnp.float32), 0.25, 1.75).astype(jnp.bfloat16)
    up_weight = scatter_about(seeds[11], (EXPERTS, D, HID), D ** -0.5, 0.125, ((0, 32), (2, 8)))
    down_weight = scatter_about(seeds[12], (EXPERTS, HID, D), HID ** -0.5, 0.09375, ((0, 32), (1, 8)))
    return {"layer_in": layer_in, "queries": queries, "fresh_entries": fresh_entries, "cross_queries": cross_queries, "past_cache": past_cache, "encoder_states": encoder_states, "source_lengths": source_lengths, "parents": parents, "expert_ids": expert_ids, "gate_weights": gate_weights, "norm_gain": norm_gain, "up_weight": up_weight, "down_weight": down_weight}


def attend(query_rows, key_rows, value_rows, valid_mask):
    row_count, key_count = (key_rows.shape[0], key_rows.shape[1])
    query_wide = query_rows.reshape(row_count, HEADS, DH).astype(jnp.float32)
    key_wide = key_rows.reshape(row_count, key_count, HEADS, DH).astype(jnp.float32)
    value_wide = value_rows.reshape(row_count, key_count, HEADS, DH).astype(jnp.float32)
    scores = jnp.einsum('rhd,rphd->rhp', query_wide, key_wide) / jnp.sqrt(jnp.float32(DH))
    scores = jnp.where(valid_mask[:, None, :], scores, -jnp.inf)
    highest = lax.optimization_barrier(jnp.max(scores, axis=-1, keepdims=True))
    raised = jnp.exp(scores - highest)
    weights = (raised / lax.optimization_barrier(jnp.sum(raised, axis=-1, keepdims=True))).astype(jnp.bfloat16)
    weights = lax.optimization_barrier(weights).astype(jnp.float32)
    return jnp.einsum('rhp,rphd->rhd', weights, value_wide).reshape(row_count, HEADS * DH)

def reference(layer_in, queries, fresh_entries, cross_queries, past_cache, encoder_states, source_lengths, parents, expert_ids, gate_weights, norm_gain, up_weight, down_weight):
    cache_now = past_cache
    states = []
    for step_index in range(STEPS):
        reordered = jax.vmap(lambda rows_all, order_rows: rows_all[order_rows])(cache_now, parents[step_index])
        extended = jnp.concatenate([reordered, fresh_entries[step_index][:, :, None, :]], axis=2)

        def one_group(pieces):
            extended_group, query_group, cross_group, encoder_group, length_group = pieces
            key_total = extended_group.shape[1]
            all_valid = jnp.ones((GROUP_ROWS, key_total), dtype=bool)
            self_out = attend(query_group, extended_group[:, :, :D], extended_group[:, :, D:], all_valid)
            encoder_rows = jnp.repeat(encoder_group, BEAM, axis=0)
            row_lengths = jnp.repeat(length_group, BEAM)
            cross_valid = jnp.arange(SRC)[None, :] < row_lengths[:, None]
            cross_out = attend(cross_group, encoder_rows[:, :, :D], encoder_rows[:, :, D:], cross_valid)
            return self_out + cross_out
        attended = lax.map(one_group, (extended, queries[step_index], cross_queries[step_index], encoder_states, source_lengths))
        states.append(layer_in[step_index].astype(jnp.float32) + attended)
        cache_now = extended
    residual_state = jnp.stack(states)
    centered = residual_state - lax.optimization_barrier(jnp.mean(residual_state, axis=-1, keepdims=True))
    variance = lax.optimization_barrier(jnp.mean(centered * centered, axis=-1, keepdims=True))
    normed = (centered * lax.rsqrt(variance + 1e-05) * norm_gain.astype(jnp.float32)).astype(jnp.bfloat16)
    flat_rows = normed.reshape(-1, D)
    total_rows = flat_rows.shape[0]
    flat_ids = expert_ids.reshape(total_rows, 2)
    flat_gates = gate_weights.reshape(total_rows, 2)
    room_size = CAP * STEPS * GROUPS

    def per_expert(running, expert):
        matches = flat_ids == expert
        chosen = jnp.any(matches, axis=1)
        share_weight = lax.optimization_barrier(jnp.sum(jnp.where(matches, flat_gates, 0.0), axis=1))
        slot_place = jnp.cumsum(chosen.astype(jnp.int32)) - 1
        slot_place = jnp.where(chosen, slot_place, room_size).astype(jnp.int32)
        packed = jnp.zeros((room_size, D), jnp.bfloat16).at[slot_place].set(flat_rows, mode='drop')
        inner_act = jax.nn.relu(jnp.dot(packed, up_weight[expert], preferred_element_type=jnp.float32)).astype(jnp.bfloat16)
        result = jnp.dot(inner_act, down_weight[expert], preferred_element_type=jnp.float32)
        gathered = result[jnp.minimum(slot_place, room_size - 1)]
        return (running + share_weight[:, None] * gathered, None)
    mixture, _ = lax.scan(per_expert, jnp.zeros((total_rows, D), jnp.float32), jnp.arange(EXPERTS, dtype=jnp.int32))
    layer_out = (residual_state.reshape(total_rows, D) + mixture).reshape(residual_state.shape).astype(jnp.bfloat16)
    return (layer_out, cache_now)
```

```python
import functools

import jax
import jax.numpy as jnp
from jax import lax
from jax.experimental import pallas as pl
from jax.experimental.pallas import tpu as pltpu
from jax.sharding import PartitionSpec as P

HEADS = 16
DH = 128
CAP = 4
STEPS = 2
SLOTS = 8
BEAM = 4
NB = 8
ROWS = NB * SLOTS
PER = 2 * CAP
POS = 16
MESH = pl.DeviceIdType.MESH
F32 = jnp.float32
BF16 = jnp.bfloat16


def iota(shape, dim):
    return lax.broadcasted_iota(jnp.int32, shape, dim)


def plan_kernel(par_ref, out_ref):
    n = ROWS
    row_i, col_i = iota((n, n), 1), iota((n, n), 0)
    rowf, colf = row_i.astype(F32), col_i.astype(F32)
    dev_r, dev_c = jnp.floor(rowf * 0.125), jnp.floor(colf * 0.125)
    eye = (row_i == col_i).astype(F32)
    tri = jnp.where((row_i < col_i) & (dev_r == dev_c), 1.0, 0.0)

    def across(x):
        return jnp.broadcast_to(jnp.sum(x, axis=1, keepdims=True), (n, n))

    def down(x):
        return jnp.broadcast_to(jnp.sum(x, axis=0, keepdims=True), (n, n))

    def to_col(r):
        return across(eye * r)

    def to_row(c):
        return down(eye * c)

    def step(par):
        pr = jnp.broadcast_to(par.astype(F32), (n, n))
        pc = to_col(pr)
        hot = jnp.where(colf == pr, 1.0, 0.0)
        cross_r = jnp.where(jnp.floor(pr * 0.125) != dev_r, 1.0, 0.0)
        cross_c = to_col(cross_r)
        leave_c = across(hot * cross_r)
        leave_r = to_row(leave_c)
        pool_c = dev_c * 2 + across(tri * leave_r)
        src_c = to_col(down(hot * pool_c))
        arank_c = across(tri * cross_r)
        place = jnp.where(rowf == dev_c * 2 + arank_c, cross_c, 0.0)
        leave = jnp.where(rowf == pool_c, leave_c, 0.0)
        local_r = pr - 8 * jnp.floor(pr * 0.125)
        ext = jnp.where(cross_r > 0, 8 + to_row(arank_c), local_r)
        return pc, hot, cross_c, pool_c, src_c, place, leave, ext

    p0c, hot0, cross0, pool0, src0, place0, leave0, ext0 = step(par_ref[0:1, :])
    p1c, hot1, cross1, pool1, src1, place1, leave1, ext1 = step(par_ref[1:2, :])
    slot_c = colf - 8 * dev_c
    from_c = jnp.where(cross0 > 0, src0, 16 + pool1)
    kept_c = jnp.where(cross0 > 0, 0.0, p0c - 8 * jnp.floor(p0c * 0.125))
    srcc1 = to_col(down(hot1 * from_c))
    tables = (
        ext0,
        ext1,
        down(leave0 * slot_c),
        down(leave1 * kept_c),
        down(leave1 * slot_c),
        down(place0 * src0),
        down(place1 * srcc1),
        down(place1 * src1),
    )
    for k, table in enumerate(tables):
        out_ref[k : k + 1, :] = table[0:1, :].astype(jnp.int32)


def head_mask(rows):
    head = iota((rows, HEADS, HEADS * DH), 1)
    column = iota((rows, HEADS, HEADS * DH), 2) // DH
    return (head == column).astype(F32)


def attend(q, keys, values, valid):
    d = HEADS * DH
    mask = head_mask(SLOTS)
    spread = (jnp.broadcast_to(q[:, None, :], (SLOTS, HEADS, d)) * mask).reshape(SLOTS * HEADS, d)
    scores = lax.dot_general(
        spread.astype(BF16), keys, (((1,), (1,)), ((), ())), preferred_element_type=F32
    ) * (1.0 / DH**0.5)
    scores = jnp.where(valid, scores, -1e30)
    raised = jnp.where(valid, jnp.exp(scores - jnp.max(scores, axis=1, keepdims=True)), 0.0)
    weights = (raised / jnp.sum(raised, axis=1, keepdims=True)).astype(BF16)
    out = jnp.dot(weights, values, preferred_element_type=F32)
    return jnp.sum(out.reshape(SLOTS, HEADS, d) * mask, axis=1)


def layer_kernel(
    ne,
    tbl, lens, layer_in, queries, fresh, cross_q, cache, enc, ids, gates, gain, up_hbm, down_hbm,
    layer_out, cache_out,
    wup, wdn, freshf, st_a, pool0, pool1, st_b, cvx, ebuf, ext1, cross_s, resid,
    pack_p, gate_hi, gate_lo, hsend, hrecv, psend, xb, hid, sib_s, sib_r, ysend, yrecv,
    rsend, rrecv, fsend, frecv, wsem, lsem, csem, bsend, brecv, agsend, agrecv, sibsend, sibrecv,
):
    b, e = lax.axis_index("batch"), lax.axis_index("expert")
    y, c = b // 2, b % 2
    sib = y * 2 + (1 - c)
    d = HEADS * DH
    kc = 2 * d // NB
    mc = d // NB
    slots = ne * PER

    def peer_y(q):
        return lax.rem(y + q, 4)

    barrier = pltpu.get_barrier_semaphore()

    def greet_b(k, _):
        pl.semaphore_signal(
            barrier, inc=1, device_id=(lax.rem(b + k, NB), e), device_id_type=MESH
        )
        return 0

    def greet_e(k, _):
        pl.semaphore_signal(
            barrier, inc=1, device_id=(b, lax.rem(e + k, ne)), device_id_type=MESH
        )
        return 0

    lax.fori_loop(1, NB, greet_b, 0)
    lax.fori_loop(1, ne, greet_e, 0)

    up_copy = pltpu.make_async_copy(up_hbm, wup, wsem.at[0])
    down_copy = pltpu.make_async_copy(down_hbm, wdn, wsem.at[1])
    up_copy.start()
    down_copy.start()

    def local(src, dst):
        copy = pltpu.make_async_copy(src, dst, lsem)
        copy.start()
        copy.wait()

    def wait_bytes(ref, sem):
        pltpu.make_async_copy(ref, ref, sem).wait()

    position = iota((POS, 2 * d), 0)

    def to16(rows14):
        pad = jnp.zeros((POS - rows14.shape[0], rows14.shape[1]), F32)
        return jnp.concatenate([rows14.astype(F32), pad], axis=0)

    for t in range(STEPS):
        for r in range(SLOTS):
            freshf[t, r] = fresh[t, r : r + 1, :].astype(F32)
    for j in range(2):
        st_a[0, j] = to16(cache[tbl[2, b * 2 + j]]).astype(BF16)
        entry = jnp.broadcast_to(freshf[0, tbl[4, b * 2 + j]], (POS, 2 * d))
        st_a[1, j] = jnp.where(
            position == 14, entry, to16(cache[tbl[3, b * 2 + j]])
        ).astype(BF16)

    pl.semaphore_wait(barrier, NB - 1 + ne - 1)

    pools = (pool0, pool1)
    landing = (cvx, ebuf)

    def send_a(t):
        def one(k, _):
            to = lax.rem(b + k, NB)
            pltpu.make_async_remote_copy(
                st_a.at[t, :, :, pl.ds(pl.multiple_of(to * kc, kc), kc)],
                pools[t].at[pl.ds(b * 2, 2)],
                bsend.at[t, 0], brecv.at[t, 0], device_id=(to, e), device_id_type=MESH,
            ).start()
            return 0

        lax.fori_loop(1, NB, one, 0)
        local(st_a.at[t, :, :, pl.ds(pl.multiple_of(b * kc, kc), kc)], pools[t].at[pl.ds(b * 2, 2)])

    def send_b(t):
        def one(k, _):
            to = lax.rem(b + k, NB)
            pltpu.make_async_remote_copy(
                st_b.at[t, pl.ds(to * 2, 2)],
                landing[t].at[pl.ds(SLOTS, 2), :, pl.ds(pl.multiple_of(b * kc, kc), kc)],
                bsend.at[t, 1], brecv.at[t, 1], device_id=(to, e), device_id_type=MESH,
            ).start()
            return 0

        lax.fori_loop(1, NB, one, 0)
        local(
            st_b.at[t, pl.ds(b * 2, 2)],
            landing[t].at[pl.ds(SLOTS, 2), :, pl.ds(pl.multiple_of(b * kc, kc), kc)],
        )

    send_a(0)
    send_a(1)

    for r in range(SLOTS):
        cvx[r] = to16(cache[r]).astype(BF16)
    own_s = iota((SLOTS * HEADS, BEAM * 0 + 64), 0) // (HEADS * BEAM)
    key_i = iota((SLOTS * HEADS, 64), 1)
    limit = jnp.where(own_s == 0, lens[0, 0], lens[0, 1])
    cross_valid = (key_i // 32 == own_s) & (key_i % 32 < limit)
    enc_k = enc[:, :, :d].reshape(64, d)
    enc_v = enc[:, :, d:].reshape(64, d)
    for t in range(STEPS):
        cross_s[t] = attend(cross_q[t].astype(F32), enc_k, enc_v, cross_valid)

    lane = iota((ROWS, slots), 1)
    expert = lane // PER * 2 + lane % PER // CAP
    place = (lane % CAP).astype(F32)
    earlier = jnp.where(iota((ROWS, ROWS), 1) < iota((ROWS, ROWS), 0), 1.0, 0.0).astype(BF16)
    for t in range(STEPS):
        first = jnp.where(ids[t, :, 0:1] == expert, 1.0, 0.0)
        second = jnp.where(ids[t, :, 1:2] == expert, 1.0, 0.0)
        named = first + second
        rank = jnp.dot(earlier, named.astype(BF16), preferred_element_type=F32)
        chosen = jnp.where(rank == place, named, 0.0)
        pack_p[t] = jnp.transpose(chosen).astype(BF16)
        weight = chosen * (first * gates[t, :, 0:1] + second * gates[t, :, 1:2])
        high = weight.astype(BF16)
        gate_hi[t] = high
        gate_lo[t] = (weight - high.astype(F32)).astype(BF16)

    def stage_b(t):
        for m in range(2 * NB):
            if t == 0:
                st_b[0, m] = pool0[tbl[5, m]]
            else:
                at = tbl[6, m]
                old = pool0[jnp.minimum(at, 15)].astype(F32)
                new = pool1[jnp.maximum(at - 16, 0)].astype(F32)
                entry = pool1[tbl[7, m]].astype(F32)
                kept = jnp.where(iota((POS, kc), 0) * 0 + at < 16, old, new)
                st_b[1, m] = jnp.where(iota((POS, kc), 0) == 14, entry, kept).astype(BF16)

    for t in range(STEPS):
        wait_bytes(pools[t].at[pl.ds(0, 14)], brecv.at[t, 0])
        stage_b(t)
        send_b(t)

    own_r = iota((SLOTS * HEADS, SLOTS * POS), 0) // HEADS
    self_key = iota((SLOTS * HEADS, SLOTS * POS), 1)

    def attention(t):
        wait_bytes(st_b.at[t, pl.ds(0, 14)], brecv.at[t, 1])
        if t == 0:
            for r in range(SLOTS):
                row = cvx[tbl[0, b * SLOTS + r]].astype(F32)
                entry = jnp.broadcast_to(freshf[0, r], (POS, 2 * d))
                ebuf[r] = jnp.where(position == 14, entry, row).astype(BF16)
            held = ebuf
        else:
            for r in range(SLOTS):
                row = ebuf[tbl[1, b * SLOTS + r]].astype(F32)
                entry = jnp.broadcast_to(freshf[1, r], (POS, 2 * d))
                ext1[r] = jnp.where(position == 15, entry, row).astype(BF16)
            held = ext1
            pltpu.make_async_copy(ext1, cache_out, csem).start()
        valid = (self_key // POS == own_r) & (self_key % POS < 15 + t)
        keys = held[0:SLOTS, :, :d].reshape(SLOTS * POS, d)
        values = held[0:SLOTS, :, d:].reshape(SLOTS * POS, d)
        state = (
            layer_in[t].astype(F32)
            + attend(queries[t].astype(F32), keys, values, valid)
            + cross_s[t]
        )
        resid[t] = state
        centered = state - jnp.mean(state, axis=1, keepdims=True)
        variance = jnp.mean(centered * centered, axis=1, keepdims=True)
        normed = centered * lax.rsqrt(variance + 1e-05) * gain[...].astype(F32)
        for j in range(NB):
            hsend[t, j] = normed[:, j * mc : (j + 1) * mc]

        def one(k, _):
            to = lax.rem(b + k, NB)
            pltpu.make_async_remote_copy(
                hsend.at[t, to], hrecv.at[t, b],
                bsend.at[t, 2], brecv.at[t, 2], device_id=(to, e), device_id_type=MESH,
            ).start()
            return 0

        lax.fori_loop(1, NB, one, 0)
        hrecv[t, b] = hsend[t, b]

    half = mc // 2

    def halves(x):
        left = x[:, :half].reshape(ne, PER, half)
        right = x[:, half:].reshape(ne, PER, half)
        return jnp.concatenate([left, right], axis=1).astype(BF16)

    def whole(x):
        x = x.astype(F32)
        left = x[:, :PER].reshape(slots, half)
        right = x[:, PER:].reshape(slots, half)
        return jnp.concatenate([left, right], axis=1).astype(BF16)

    def dispatch(t):
        wait_bytes(hrecv.at[t, pl.ds(0, 7)], brecv.at[t, 2])
        rows = hrecv[t].reshape(ROWS, mc).astype(BF16)
        psend[t] = halves(jnp.dot(pack_p[t], rows, preferred_element_type=F32))

        def one(k, _):
            to = lax.rem(e + k, ne)
            pltpu.make_async_remote_copy(
                psend.at[t, to], xb.at[t, b, e],
                bsend.at[t, 3], brecv.at[t, 3], device_id=(b, to), device_id_type=MESH,
            ).start()
            return 0

        lax.fori_loop(1, ne, one, 0)
        xb[t, b, e] = psend[t, e]

    def ag_copy(t, which, block, to):
        return pltpu.make_async_remote_copy(
            xb.at[t, block], xb.at[t, block],
            agsend.at[t, which], agrecv.at[t, which], device_id=(to, e), device_id_type=MESH,
        )

    def gather_start(t):
        wait_bytes(psend.at[t, pl.ds(0, ne - 1)], brecv.at[t, 3])
        for q in (1, 3, 2):
            ag_copy(t, q, b, peer_y(q) * 2 + c).start()
        ag_copy(t, 0, b, sib).start()

    def up_part(t, block, first):
        x = whole(xb[t, block])
        at = pl.ds(pl.multiple_of(block * mc, mc), mc)
        for k in range(2):
            part = jnp.dot(x, wup[k, at, :], preferred_element_type=F32)
            if first:
                hid[k] = part
            else:
                hid[k] += part

    def gather_compute(t):
        up_part(t, b, True)
        for q in (1, 3, 2):
            block = peer_y(4 - q) * 2 + c
            ag_copy(t, q, block, sib).wait_recv()
            ag_copy(t, 3 + q, block, sib).start()
            if q == 1:
                ag_copy(t, 0, sib, sib).wait_recv()
                up_part(t, sib, False)
            up_part(t, block, False)
        for q in (1, 3, 2):
            block = peer_y(4 - q) * 2 + (1 - c)
            ag_copy(t, 3 + q, block, sib).wait_recv()
            up_part(t, block, False)

    def down_part(t, block, acts):
        at = pl.ds(pl.multiple_of(block * mc, mc), mc)
        return jnp.dot(acts[0], wdn[0, :, at], preferred_element_type=F32) + jnp.dot(
            acts[1], wdn[1, :, at], preferred_element_type=F32
        )

    def sib_copy(t, q):
        return pltpu.make_async_remote_copy(
            sib_s.at[t, q], sib_r.at[t, q],
            sibsend.at[t, q], sibrecv.at[t, q], device_id=(sib, e), device_id_type=MESH,
        )

    def y_copy(t, q):
        return pltpu.make_async_remote_copy(
            ysend.at[t, q - 1], yrecv.at[t, q - 1],
            sibsend.at[t, 3 + q], sibrecv.at[t, 3 + q],
            device_id=(peer_y(q) * 2 + c, e), device_id_type=MESH,
        )

    def scatter_start(t):
        own = iota((slots, hid.shape[2]), 0) % PER // CAP
        acts = [
            jnp.where(own == k, jnp.maximum(hid[k], 0.0), 0.0).astype(BF16) for k in range(2)
        ]
        for q in (1, 3, 2, 0):
            sib_s[t, q] = down_part(t, peer_y(q) * 2 + (1 - c), acts)
            sib_copy(t, q).start()
        for q in (1, 3, 2):
            part = down_part(t, peer_y(q) * 2 + c, acts)
            sib_copy(t, q).wait_recv()
            ysend[t, q - 1] = (part + sib_r[t, q]).astype(BF16)
            y_copy(t, q).start()
        part = down_part(t, b, acts)
        sib_copy(t, 0).wait_recv()
        sib_r[t, 0] = part + sib_r[t, 0]

    def give_back(t):
        total = sib_r[t, 0]
        for q in (1, 3, 2):
            y_copy(t, q).wait_recv()
            total = total + yrecv[t, q - 1].astype(F32)
        rsend[t] = halves(total)

        def one(k, _):
            to = lax.rem(e + k, ne)
            pltpu.make_async_remote_copy(
                rsend.at[t, to], rrecv.at[t, e],
                bsend.at[t, 4], brecv.at[t, 4], device_id=(b, to), device_id_type=MESH,
            ).start()
            return 0

        lax.fori_loop(1, ne, one, 0)
        rrecv[t, e] = rsend[t, e]

    def combine(t):
        wait_bytes(rsend.at[t, pl.ds(0, ne - 1)], brecv.at[t, 4])
        came = whole(rrecv[t])
        mixed = jnp.dot(gate_hi[t], came, preferred_element_type=F32) + jnp.dot(
            gate_lo[t], came, preferred_element_type=F32
        )
        fsend[t] = mixed.reshape(NB, SLOTS, mc)

        def one(k, _):
            to = lax.rem(b + k, NB)
            pltpu.make_async_remote_copy(
                fsend.at[t, to], frecv.at[t, b],
                bsend.at[t, 5], brecv.at[t, 5], device_id=(to, e), device_id_type=MESH,
            ).start()
            return 0

        lax.fori_loop(1, NB, one, 0)
        frecv[t, b] = fsend[t, b]

    def finish(t):
        wait_bytes(frecv.at[t, pl.ds(0, 7)], brecv.at[t, 5])
        for j in range(NB):
            cols = slice(j * mc, (j + 1) * mc)
            layer_out[t, :, cols] = (resid[t, :, cols] + frecv[t, j]).astype(BF16)

    attention(0)
    attention(1)
    dispatch(0)
    dispatch(1)
    gather_start(0)
    up_copy.wait()
    gather_start(1)
    gather_compute(0)
    down_copy.wait()
    scatter_start(0)
    gather_compute(1)
    give_back(0)
    scatter_start(1)
    combine(0)
    give_back(1)
    finish(0)
    combine(1)
    finish(1)

    for t in range(STEPS):
        wait_bytes(st_b.at[t, pl.ds(0, 14)], bsend.at[t, 0])
        wait_bytes(st_b.at[t, pl.ds(0, 14)], bsend.at[t, 1])
        wait_bytes(hsend.at[t, pl.ds(0, 7)], bsend.at[t, 2])
        wait_bytes(psend.at[t, pl.ds(0, ne - 1)], bsend.at[t, 3])
        wait_bytes(rsend.at[t, pl.ds(0, ne - 1)], bsend.at[t, 4])
        wait_bytes(fsend.at[t, pl.ds(0, 7)], bsend.at[t, 5])
        for which in range(7):
            ag_copy(t, which, b, sib).wait_send()
        for q in range(4):
            sib_copy(t, q).wait_send()
        for q in range(1, 4):
            y_copy(t, q).wait_send()
    pltpu.make_async_copy(ext1, cache_out, csem).wait()


def shards(
    layer_in, queries, fresh_entries, cross_queries, past_cache, encoder_states, source_lengths,
    parents, expert_ids, gate_weights, norm_gain, up_weight, down_weight,
):
    ne = lax.axis_size("expert")
    d = HEADS * DH
    mc = d // NB
    half = mc // 2
    kc = 2 * d // NB
    slots = ne * PER
    hs = up_weight.shape[2]
    tables = pl.pallas_call(
        plan_kernel,
        out_shape=jax.ShapeDtypeStruct((8, ROWS), jnp.int32),
        in_specs=[pl.BlockSpec(memory_space=pltpu.VMEM)],
        out_specs=pl.BlockSpec(memory_space=pltpu.VMEM),
        name="plan",
    )(parents[:, 0])
    vmem = pl.BlockSpec(memory_space=pltpu.VMEM)
    smem = pl.BlockSpec(memory_space=pltpu.SMEM)
    hbm = pl.BlockSpec(memory_space=pl.ANY)
    dma = pltpu.SemaphoreType.DMA
    layer_out, cache_out = pl.pallas_call(
        functools.partial(layer_kernel, ne),
        out_shape=(
            jax.ShapeDtypeStruct((STEPS, SLOTS, d), BF16),
            jax.ShapeDtypeStruct((SLOTS, POS, 2 * d), BF16),
        ),
        in_specs=[smem, smem] + [vmem] * 9 + [hbm, hbm],
        out_specs=(vmem, hbm),
        scratch_shapes=[
            pltpu.VMEM((2, d, hs), BF16),
            pltpu.VMEM((2, hs, d), BF16),
            pltpu.VMEM((STEPS, SLOTS, 1, 2 * d), F32),
            pltpu.VMEM((STEPS, 2, POS, 2 * d), BF16),
            pltpu.VMEM((16, POS, kc), BF16),
            pltpu.VMEM((16, POS, kc), BF16),
            pltpu.VMEM((STEPS, 16, POS, kc), BF16),
            pltpu.VMEM((SLOTS + 2, POS, 2 * d), BF16),
            pltpu.VMEM((SLOTS + 2, POS, 2 * d), BF16),
            pltpu.VMEM((SLOTS, POS, 2 * d), BF16),
            pltpu.VMEM((STEPS, SLOTS, d), F32),
            pltpu.VMEM((STEPS, SLOTS, d), F32),
            pltpu.VMEM((STEPS, slots, ROWS), BF16),
            pltpu.VMEM((STEPS, ROWS, slots), BF16),
            pltpu.VMEM((STEPS, ROWS, slots), BF16),
            pltpu.VMEM((STEPS, NB, SLOTS, mc), F32),
            pltpu.VMEM((STEPS, NB, SLOTS, mc), F32),
            pltpu.VMEM((STEPS, ne, 2 * PER, half), BF16),
            pltpu.VMEM((STEPS, NB, ne, 2 * PER, half), BF16),
            pltpu.VMEM((2, slots, hs), F32),
            pltpu.VMEM((STEPS, 4, slots, mc), F32),
            pltpu.VMEM((STEPS, 4, slots, mc), F32),
            pltpu.VMEM((STEPS, 3, slots, mc), BF16),
            pltpu.VMEM((STEPS, 3, slots, mc), BF16),
            pltpu.VMEM((STEPS, ne, 2 * PER, half), BF16),
            pltpu.VMEM((STEPS, ne, 2 * PER, half), BF16),
            pltpu.VMEM((STEPS, NB, SLOTS, mc), F32),
            pltpu.VMEM((STEPS, NB, SLOTS, mc), F32),
            dma((2,)),
            dma,
            dma,
            dma((STEPS, 6)),
            dma((STEPS, 6)),
            dma((STEPS, 7)),
            dma((STEPS, 7)),
            dma((STEPS, 7)),
            dma((STEPS, 7)),
        ],
        compiler_params=pltpu.CompilerParams(
            collective_id=1, has_side_effects=True, vmem_limit_bytes=56 * 2**20
        ),
        cost_estimate=pl.CostEstimate(
            flops=4 * STEPS * slots * d * hs * 2, bytes_accessed=12 * 2**20, transcendentals=0
        ),
        name="layer",
    )(
        tables, source_lengths, layer_in[:, 0], queries[:, 0], fresh_entries[:, 0],
        cross_queries[:, 0], past_cache[0], encoder_states[0], expert_ids[:, 0],
        gate_weights[:, 0], norm_gain[None], up_weight, down_weight,
    )
    return layer_out[:, None], cache_out[None]


def solution(mesh):
    in_specs = (
        P(None, "expert", "batch", None),
        P(None, "expert", "batch", None),
        P(None, "expert", "batch", None),
        P(None, "expert", "batch", None),
        P("expert", "batch", None, None),
        P("expert", "batch", None, None),
        P("expert", "batch"),
        P(None, "expert", None),
        P(None, "expert", None, None),
        P(None, "expert", None, None),
        P(),
        P("expert", None, "batch"),
        P("expert", "batch", None),
    )
    out_specs = (P(None, "expert", "batch", None), P("expert", "batch", None, None))
    return jax.shard_map(shards, mesh=mesh, in_specs=in_specs, out_specs=out_specs, check_vma=False)
```

```python
import functools

import jax
import jax.numpy as jnp
from jax import lax
from jax.experimental import pallas as pl
from jax.experimental.pallas import tpu as pltpu
from jax.sharding import PartitionSpec as P

HEADS = 16
DH = 128
CAP = 4
STEPS = 2
SLOTS = 8
BEAM = 4
CACHE = 14
NB = 8
ROWS = NB * SLOTS
PER = 2 * CAP
POS = 16
MESH = pl.DeviceIdType.MESH
F32 = jnp.float32
BF16 = jnp.bfloat16


def iota(shape, dim):
    return lax.broadcasted_iota(jnp.int32, shape, dim)


def hot(mask):
    return jnp.where(mask, 1.0, 0.0).astype(BF16)


def dot(x, y):
    return jnp.dot(x, y, preferred_element_type=F32)


def move_plan(par):
    n = ROWS
    row, col = iota((n, n), 1), iota((n, n), 0)
    dev_r, dev_c = row // SLOTS, col // SLOTS
    before = jnp.where((row < col) & (dev_r == dev_c), 1.0, 0.0)

    def across(x):
        return jnp.broadcast_to(jnp.sum(x, axis=1, keepdims=True), (n, n))

    def down(x):
        return jnp.broadcast_to(jnp.sum(x, axis=0, keepdims=True), (n, n))

    eye = jnp.where(row == col, 1.0, 0.0)
    par_r = jnp.broadcast_to(par, (n, n))
    takes = jnp.where(col == par_r, 1.0, 0.0)
    cross_r = jnp.where(par_r // SLOTS != dev_r, 1.0, 0.0)
    cross_c = across(eye * cross_r)
    leave_c = across(takes * cross_r)
    leave_r = down(eye * leave_c)
    give_c = across(before * leave_r) + 2.0 * dev_c.astype(F32)
    give_r = down(eye * give_c)
    take_c = across(before * cross_r) + 2.0 * dev_c.astype(F32)
    take_r = down(eye * take_c)
    rowf, colf = row.astype(F32), col.astype(F32)
    given = jnp.where(rowf == give_c, leave_c, 0.0).astype(BF16)
    given_t = jnp.where(colf == give_r, leave_r, 0.0).astype(BF16)
    taken = jnp.where(rowf == take_c, cross_c, 0.0).astype(BF16)
    taken_t = jnp.where(colf == take_r, cross_r, 0.0).astype(BF16)
    takes_t = jnp.transpose(takes).astype(BF16)
    return takes_t, given, given_t, taken, taken_t


def head_mask(rows):
    head = iota((rows, HEADS, HEADS * DH), 1)
    column = iota((rows, HEADS, HEADS * DH), 2) // DH
    return (head == column).astype(F32)


def attend(q, keys, values, valid):
    d = HEADS * DH
    mask = head_mask(SLOTS)
    spread = (jnp.broadcast_to(q[:, None, :], (SLOTS, HEADS, d)) * mask).reshape(SLOTS * HEADS, d)
    scores = lax.dot_general(
        spread.astype(BF16), keys, (((1,), (1,)), ((), ())), preferred_element_type=F32
    ) * (1.0 / DH**0.5)
    scores = jnp.where(valid, scores, -1e30)
    raised = jnp.where(valid, jnp.exp(scores - jnp.max(scores, axis=1, keepdims=True)), 0.0)
    weights = (raised / jnp.sum(raised, axis=1, keepdims=True)).astype(BF16)
    out = jnp.dot(weights, values, preferred_element_type=F32)
    return jnp.sum(out.reshape(SLOTS, HEADS, d) * mask, axis=1)


def layer_kernel(
    ne,
    lens, par, layer_in, queries, fresh, cross_q, cache, enc, ids, gates, gain, up_hbm, down_hbm,
    layer_out, cache_out,
    wup, wdn, src0, src1, ext1, st_a, pool0, pool1, st_b, cross_s, resid,
    pack_p, gate_hi, gate_lo, hsend, hrecv, psend, xb, hid, sib_s, sib_r, ysend, yrecv,
    rsend, rrecv, fsend, frecv, wsem, lsem, csem, bsend, brecv, agsend, agrecv, sibsend, sibrecv,
):
    b, e = lax.axis_index("batch"), lax.axis_index("expert")
    y, c = b // 2, b % 2
    sib = y * 2 + (1 - c)
    d = HEADS * DH
    kc = 2 * d // NB
    mc = d // NB
    slots = ne * PER
    unsent, unreceived = [], {}

    def peer_y(q):
        return lax.rem(y + q, 4)

    barrier = pltpu.get_barrier_semaphore()

    def greet_b(k, _):
        pl.semaphore_signal(
            barrier, inc=1, device_id=(lax.rem(b + k, NB), e), device_id_type=MESH
        )
        return 0

    def greet_e(k, _):
        pl.semaphore_signal(
            barrier, inc=1, device_id=(b, lax.rem(e + k, ne)), device_id_type=MESH
        )
        return 0

    lax.fori_loop(1, NB, greet_b, 0)
    lax.fori_loop(1, ne, greet_e, 0)

    up_copy = pltpu.make_async_copy(up_hbm, wup, wsem.at[0])
    down_copy = pltpu.make_async_copy(down_hbm, wdn, wsem.at[1])
    up_copy.start()
    down_copy.start()

    def local(src, dst):
        copy = pltpu.make_async_copy(src, dst, lsem)
        copy.start()
        copy.wait()

    def wait_bytes(ref, sem):
        pltpu.make_async_copy(ref, ref, sem).wait()

    def to_all(axis, t, phase, make, ref):
        count = NB if axis == "batch" else ne

        def one(k, _):
            src, dst, to = make(k)
            to = (to, e) if axis == "batch" else (b, to)
            pltpu.make_async_remote_copy(
                src, dst, bsend.at[t, phase], brecv.at[t, phase], device_id=to, device_id_type=MESH
            ).start()
            return 0

        lax.fori_loop(1, count, one, 0)
        unsent.append(lambda: wait_bytes(ref, bsend.at[t, phase]))
        unreceived[t, phase] = lambda: wait_bytes(ref, brecv.at[t, phase])

    def arrive(t, phase):
        unreceived.pop((t, phase))()

    near, late = CACHE * SLOTS, CACHE * SLOTS + 2 * POS
    src0[0:near] = cache[...].astype(F32).reshape(near, 2 * d).astype(BF16)
    blank = jnp.zeros((SLOTS, 2 * d), F32)
    src0[late:] = jnp.concatenate([fresh[0].astype(F32), blank], axis=0).astype(BF16)
    src1[late + POS :] = jnp.concatenate([fresh[1].astype(F32), blank], axis=0).astype(BF16)

    same_dev = iota((ROWS, ROWS), 0) // SLOTS == iota((ROWS, ROWS), 1) // SLOTS
    own_m = hot(iota((2 * POS, ROWS), 1) == 2 * b + iota((2 * POS, ROWS), 0) // POS)
    near_c = hot(iota((ROWS, near), 0) == SLOTS * b + iota((ROWS, near), 1) % SLOTS)
    near_p = iota((2 * POS, near), 0) % POS == iota((2 * POS, near), 1) // SLOTS

    def given_rows(chosen):
        pick = dot(dot(own_m, chosen).astype(BF16), near_c)
        return dot(jnp.where(near_p, pick, 0.0).astype(BF16), src0[0:near])

    takes0, given0, given0_t, taken0, taken0_t = move_plan(par[0:1, :])
    st_a[0] = given_rows(given0_t).astype(BF16)

    pl.semaphore_wait(barrier, NB - 1 + ne - 1)

    pools = (pool0, pool1)

    def own_cols(k):
        return pl.ds(pl.multiple_of(k * kc, kc), kc)

    def own_rows(k):
        return pl.ds(pl.multiple_of(k * 2 * POS, 2 * POS), 2 * POS)

    def send_a(t):
        def make(k):
            to = lax.rem(b + k, NB)
            return st_a.at[t, :, own_cols(to)], pools[t].at[own_rows(b)], to

        to_all("batch", t, 0, make, st_b.at[t, pl.ds(0, 14 * POS)])
        local(st_a.at[t, :, own_cols(b)], pools[t].at[own_rows(b)])

    def send_b(t):
        landing = src0.at[near:late] if t == 0 else src1.at[SLOTS * POS : SLOTS * POS + 2 * POS]

        def make(k):
            to = lax.rem(b + k, NB)
            return st_b.at[t, own_rows(to)], landing.at[:, own_cols(b)], to

        to_all("batch", t, 1, make, st_b.at[t, pl.ds(0, 14 * POS)])
        local(st_b.at[t, own_rows(b)], landing.at[:, own_cols(b)])

    send_a(0)

    takes1, given1, given1_t, taken1, taken1_t = move_plan(par[1:2, :])
    kept1_t = dot(given1_t, jnp.where(same_dev, takes0.astype(F32), 0.0).astype(BF16)).astype(BF16)
    slot_c = hot(
        (iota((ROWS, POS), 0) == SLOTS * b + iota((ROWS, POS), 1)) & (iota((ROWS, POS), 1) < SLOTS)
    )
    entry = dot(dot(own_m, given1_t).astype(BF16), slot_c)
    entry = jnp.where(iota((2 * POS, POS), 0) % POS == CACHE, entry, 0.0).astype(BF16)
    st_a[1] = (given_rows(kept1_t) + dot(entry, src0[late:])).astype(BF16)

    own_s = iota((SLOTS * HEADS, 64), 0) // (HEADS * BEAM)
    key_i = iota((SLOTS * HEADS, 64), 1)
    limit = jnp.where(own_s == 0, lens[0, 0], lens[0, 1])
    cross_valid = (key_i // 32 == own_s) & (key_i % 32 < limit)
    enc_k = enc[:, :, :d].reshape(64, d)
    enc_v = enc[:, :, d:].reshape(64, d)

    def cross(t):
        cross_s[t] = attend(cross_q[t].astype(F32), enc_k, enc_v, cross_valid)

    def route(t):
        slot = iota((slots, ROWS), 0)
        owner = lax.rem(slot // PER + e, ne)
        expert = owner * 2 + slot % PER // CAP
        earlier = hot(iota((ROWS, ROWS), 0) < iota((ROWS, ROWS), 1))
        first = jnp.where(ids[t, 0:1, :] == expert, 1.0, 0.0)
        second = jnp.where(ids[t, 1:2, :] == expert, 1.0, 0.0)
        named = first + second
        rank = dot(named.astype(BF16), earlier)
        chosen = jnp.where(rank == (slot % CAP).astype(F32), named, 0.0)
        pack_p[t] = chosen.astype(BF16)
        weight = chosen * (first * gates[t, 0:1, :] + second * gates[t, 1:2, :])
        weight = jnp.transpose(weight)
        high = weight.astype(BF16)
        gate_hi[t] = high
        gate_lo[t] = (weight - high.astype(F32)).astype(BF16)

    pairs = 2 * NB * POS
    pair_m = hot(iota((pairs, ROWS), 0) // POS == iota((pairs, ROWS), 1))
    pair_mt = hot(iota((ROWS, pairs), 0) == iota((ROWS, pairs), 1) // POS)
    same_p = iota((pairs, pairs), 0) % POS == iota((pairs, pairs), 1) % POS

    def spread(small):
        wide = dot(dot(pair_m, small.astype(BF16)).astype(BF16), pair_mt)
        return jnp.where(same_p, wide, 0.0).astype(BF16)

    from0 = dot(takes0, given0).astype(BF16)
    hand0 = spread(dot(taken0_t, from0))

    def select(t, takes, taken):
        held = near if t == 0 else SLOTS * POS
        width = held + 2 * POS + POS
        shape = (SLOTS * POS, width)
        k, out_p, out_r = iota(shape, 1), iota(shape, 0) % POS, iota(shape, 0) // POS
        own_r = hot(
            iota((SLOTS * POS, ROWS), 1) == SLOTS * b + iota((SLOTS * POS, ROWS), 0) // POS
        )
        kk, cc = iota((ROWS, width), 1), iota((ROWS, width), 0)
        slot = kk % SLOTS if t == 0 else kk // POS
        at_c = hot((kk < held) & (cc == SLOTS * b + slot))
        at_m = hot((kk >= held) & (kk < held + 2 * POS) & (cc == 2 * b + (kk - held) // POS))
        picked = dot(dot(own_r, takes).astype(BF16), at_c)
        picked = picked + dot(dot(own_r, taken).astype(BF16), at_m)
        old_p = k // SLOTS if t == 0 else k % POS
        key_p = jnp.where(k < held, old_p, (k - held) % POS)
        picked = jnp.where((key_p == out_p) & (k < held + 2 * POS), picked, 0.0)
        new = (k - (held + 2 * POS) == out_r) & (out_p == CACHE + t)
        return jnp.where(new, 1.0, picked).astype(BF16)

    via1 = dot(taken1_t, takes1).astype(BF16)
    arrive(0, 0)
    st_b[0] = dot(hand0, pool0[...]).astype(BF16)
    send_b(0)
    send_a(1)
    hand1_old = spread(dot(via1, from0))
    hand1_new = spread(dot(via1, given1))
    select0 = select(0, takes0, taken0)
    cross(0)

    own_r = iota((SLOTS * HEADS, SLOTS * POS), 0) // HEADS
    self_key = iota((SLOTS * HEADS, SLOTS * POS), 1)

    def attention(t):
        arrive(t, 1)
        if t == 0:
            src1[0 : SLOTS * POS] = dot(select0, src0[...]).astype(BF16)
            held = src1
        else:
            ext1[...] = dot(select1, src1[...]).astype(BF16)
            held = ext1
            pltpu.make_async_copy(ext1, cache_out, csem).start()
            unsent.append(lambda: pltpu.make_async_copy(ext1, cache_out, csem).wait())
        valid = (self_key // POS == own_r) & (self_key % POS < CACHE + 1 + t)
        keys = held[0 : SLOTS * POS, :d]
        values = held[0 : SLOTS * POS, d:]
        state = (
            layer_in[t].astype(F32)
            + attend(queries[t].astype(F32), keys, values, valid)
            + cross_s[t]
        )
        resid[t] = state
        centered = state - jnp.mean(state, axis=1, keepdims=True)
        variance = jnp.mean(centered * centered, axis=1, keepdims=True)
        gains = gain[...].astype(F32).reshape(1, d)
        normed = centered * lax.rsqrt(variance + 1e-05) * gains
        for j in range(NB):
            hsend[t, j] = normed[:, j * mc : (j + 1) * mc]

        def make(k):
            to = lax.rem(b + k, NB)
            return hsend.at[t, to], hrecv.at[t, b], to

        to_all("batch", t, 2, make, hsend.at[t, pl.ds(0, NB - 1)])
        hrecv[t, b] = hsend[t, b]

    half = mc // 2

    def halves(x):
        left = x[:, :half].reshape(ne, PER, half)
        right = x[:, half:].reshape(ne, PER, half)
        return jnp.concatenate([left, right], axis=1).astype(BF16)

    def whole(x):
        x = x.astype(F32)
        left = x[:, :PER].reshape(slots, half)
        right = x[:, PER:].reshape(slots, half)
        return jnp.concatenate([left, right], axis=1).astype(BF16)

    def dispatch(t):
        arrive(t, 2)
        rows = hrecv[t].reshape(ROWS, mc).astype(BF16)
        psend[t] = halves(dot(pack_p[t], rows))

        def make(k):
            return psend.at[t, k], xb.at[t, b, k], lax.rem(e + k, ne)

        to_all("expert", t, 3, make, psend.at[t, pl.ds(0, ne - 1)])
        xb[t, b, 0] = psend[t, 0]

    low, high = pl.ds(0, ne // 2), pl.ds(ne // 2, ne // 2)
    every = pl.ds(0, ne)
    up_y, down_y = peer_y(1) * 2, peer_y(3) * 2
    far_y = peer_y(2) * 2

    def ag_copy(t, which):
        block, part, to = (
            (b, every, sib),
            (b, low, up_y + c),
            (b, high, down_y + c),
            (b, high, up_y + c),
            (b, low, down_y + c),
            (down_y + c, low, up_y + c),
            (up_y + c, high, down_y + c),
            (down_y + c, every, sib),
            (up_y + c, every, sib),
            (far_y + c, low, sib),
            (far_y + c, high, sib),
        )[which]
        return pltpu.make_async_remote_copy(
            xb.at[t, block, part], xb.at[t, block, part],
            agsend.at[t, which], agrecv.at[t, which], device_id=(to, e), device_id_type=MESH,
        )

    def gather_start(t):
        arrive(t, 3)
        for which in (1, 2, 3, 4, 0):
            ag_copy(t, which).start()
        for which in range(11):
            unsent.append(lambda which=which: ag_copy(t, which).wait_send())

    def gather_relay(t):
        for came, relay in ((1, 5), (2, 6)):
            ag_copy(t, came).wait_recv()
            ag_copy(t, relay).start()
        for came, pass_on in ((3, 7), (4, 8)):
            ag_copy(t, came).wait_recv()
            ag_copy(t, pass_on).start()

    def up_part(t, block, first):
        x = whole(xb[t, block])
        at = pl.ds(pl.multiple_of(block * mc, mc), mc)
        for k in range(2):
            part = jnp.dot(x, wup[k, at, :], preferred_element_type=F32)
            if first:
                hid[k] = part
            else:
                hid[k] += part

    def gather_compute(t):
        up_part(t, b, True)
        ag_copy(t, 0).wait_recv()
        up_part(t, sib, False)
        up_part(t, down_y + c, False)
        up_part(t, up_y + c, False)
        for came, pass_on in ((5, 9), (6, 10)):
            ag_copy(t, came).wait_recv()
            ag_copy(t, pass_on).start()
        ag_copy(t, 7).wait_recv()
        up_part(t, down_y + 1 - c, False)
        ag_copy(t, 8).wait_recv()
        up_part(t, up_y + 1 - c, False)
        up_part(t, far_y + c, False)
        ag_copy(t, 9).wait_recv()
        ag_copy(t, 10).wait_recv()
        up_part(t, far_y + 1 - c, False)

    def down_part(t, block, acts):
        at = pl.ds(pl.multiple_of(block * mc, mc), mc)
        return jnp.dot(acts[0], wdn[0, :, at], preferred_element_type=F32) + jnp.dot(
            acts[1], wdn[1, :, at], preferred_element_type=F32
        )

    def sib_copy(t, q):
        return pltpu.make_async_remote_copy(
            sib_s.at[t, q], sib_r.at[t, q],
            sibsend.at[t, q], sibrecv.at[t, q], device_id=(sib, e), device_id_type=MESH,
        )

    def y_copy(t, which):
        to = (up_y, down_y, up_y, down_y, up_y, down_y)[which] + c
        return pltpu.make_async_remote_copy(
            ysend.at[t, which], yrecv.at[t, which],
            sibsend.at[t, 4 + which], sibrecv.at[t, 4 + which],
            device_id=(to, e), device_id_type=MESH,
        )

    first, second = slice(0, slots // 2), slice(slots // 2, slots)

    def y_send(t, which, part):
        ysend[t, which] = part.astype(BF16)
        y_copy(t, which).start()

    def scatter_start(t):
        for q in range(4):
            unsent.append(lambda q=q: sib_copy(t, q).wait_send())
        for which in range(6):
            unsent.append(lambda which=which: y_copy(t, which).wait_send())
        own = iota((slots, hid.shape[2]), 0) % PER // CAP
        acts = [
            jnp.where(own == k, jnp.maximum(hid[k], 0.0), 0.0).astype(BF16) for k in range(2)
        ]
        def for_sib(q):
            sib_s[t, q] = down_part(t, peer_y(q) * 2 + (1 - c), acts)
            sib_copy(t, q).start()

        for_sib(2)
        for q, after in ((2, 1), (1, 3), (3, 0), (0, None)):
            if after is not None:
                for_sib(after)
            part = down_part(t, peer_y(q) * 2 + c, acts)
            sib_copy(t, q).wait_recv()
            part = part + sib_r[t, q]
            if q == 2:
                y_send(t, 0, part[first])
                y_send(t, 1, part[second])
            elif q == 1:
                y_send(t, 2, part[second])
                sib_r[t, 1, first] = part[first]
            elif q == 3:
                y_send(t, 3, part[first])
                sib_r[t, 3, second] = part[second]
            else:
                sib_r[t, 0] = part

    def scatter_relay(t):
        y_copy(t, 0).wait_recv()
        y_send(t, 4, sib_r[t, 1, first] + yrecv[t, 0].astype(F32))
        y_copy(t, 1).wait_recv()
        y_send(t, 5, sib_r[t, 3, second] + yrecv[t, 1].astype(F32))

    def give_back(t):
        for which in range(2, 6):
            y_copy(t, which).wait_recv()
        upper = sib_r[t, 0, first] + yrecv[t, 3].astype(F32) + yrecv[t, 4].astype(F32)
        lower = sib_r[t, 0, second] + yrecv[t, 2].astype(F32) + yrecv[t, 5].astype(F32)
        total = jnp.concatenate([upper, lower], axis=0)
        rsend[t] = halves(total)

        def make(k):
            return rsend.at[t, k], rrecv.at[t, k], lax.rem(e - k + ne, ne)

        to_all("expert", t, 4, make, rsend.at[t, pl.ds(0, ne - 1)])
        rrecv[t, 0] = rsend[t, 0]

    def combine(t):
        arrive(t, 4)
        came = whole(rrecv[t])
        mixed = jnp.dot(gate_hi[t], came, preferred_element_type=F32) + jnp.dot(
            gate_lo[t], came, preferred_element_type=F32
        )
        fsend[t] = mixed.reshape(NB, SLOTS, mc)

        def make(k):
            to = lax.rem(b + k, NB)
            return fsend.at[t, to], frecv.at[t, b], to

        to_all("batch", t, 5, make, fsend.at[t, pl.ds(0, NB - 1)])
        frecv[t, b] = fsend[t, b]

    def finish(t):
        arrive(t, 5)
        for j in range(NB):
            cols = slice(j * mc, (j + 1) * mc)
            layer_out[t, :, cols] = (resid[t, :, cols] + frecv[t, j]).astype(BF16)

    attention(0)
    arrive(1, 0)
    st_b[1] = (dot(hand1_old, pool0[...]) + dot(hand1_new, pool1[...])).astype(BF16)
    send_b(1)
    route(0)
    dispatch(0)
    select1 = select(1, takes1, taken1)
    cross(1)
    attention(1)
    route(1)
    gather_start(0)
    dispatch(1)
    up_copy.wait()
    gather_relay(0)
    gather_start(1)
    gather_compute(0)
    down_copy.wait()
    scatter_start(0)
    gather_relay(1)
    scatter_relay(0)
    gather_compute(1)
    scatter_start(1)
    give_back(0)
    scatter_relay(1)
    give_back(1)
    combine(0)
    finish(0)
    combine(1)
    finish(1)

    for done in unsent:
        done()


def emit_kernel(layer_in, cache_in, layer_out, cache_out, sem):
    copies = [
        pltpu.make_async_copy(cache_in, cache_out, sem.at[0]),
        pltpu.make_async_copy(layer_in, layer_out, sem.at[1]),
    ]
    for copy in copies:
        copy.start()
    for copy in copies:
        copy.wait()


def shards(
    layer_in, queries, fresh_entries, cross_queries, past_cache, encoder_states, source_lengths,
    parents, expert_ids, gate_weights, norm_gain, up_weight, down_weight,
):
    ne = lax.axis_size("expert")
    d = HEADS * DH
    mc = d // NB
    half = mc // 2
    kc = 2 * d // NB
    slots = ne * PER
    hs = up_weight.shape[2]
    vmem = pl.BlockSpec(memory_space=pltpu.VMEM)
    smem = pl.BlockSpec(memory_space=pltpu.SMEM)
    hbm = pl.BlockSpec(memory_space=pl.ANY)
    dma = pltpu.SemaphoreType.DMA
    layer_out, cache_out = pl.pallas_call(
        functools.partial(layer_kernel, ne),
        out_shape=(
            jax.ShapeDtypeStruct((STEPS, SLOTS, d), BF16),
            jax.ShapeDtypeStruct((SLOTS * POS, 2 * d), BF16),
        ),
        in_specs=[smem] + [vmem] * 10 + [hbm, hbm],
        out_specs=(vmem, hbm),
        scratch_shapes=[
            pltpu.VMEM((2, d, hs), BF16),
            pltpu.VMEM((2, hs, d), BF16),
            pltpu.VMEM((CACHE * SLOTS + 2 * POS + POS, 2 * d), BF16),
            pltpu.VMEM((SLOTS * POS + 2 * POS + POS, 2 * d), BF16),
            pltpu.VMEM((SLOTS * POS, 2 * d), BF16),
            pltpu.VMEM((STEPS, 2 * POS, 2 * d), BF16),
            pltpu.VMEM((2 * NB * POS, kc), BF16),
            pltpu.VMEM((2 * NB * POS, kc), BF16),
            pltpu.VMEM((STEPS, 2 * NB * POS, kc), BF16),
            pltpu.VMEM((STEPS, SLOTS, d), F32),
            pltpu.VMEM((STEPS, SLOTS, d), F32),
            pltpu.VMEM((STEPS, slots, ROWS), BF16),
            pltpu.VMEM((STEPS, ROWS, slots), BF16),
            pltpu.VMEM((STEPS, ROWS, slots), BF16),
            pltpu.VMEM((STEPS, NB, SLOTS, mc), F32),
            pltpu.VMEM((STEPS, NB, SLOTS, mc), F32),
            pltpu.VMEM((STEPS, ne, 2 * PER, half), BF16),
            pltpu.VMEM((STEPS, NB, ne, 2 * PER, half), BF16),
            pltpu.VMEM((2, slots, hs), F32),
            pltpu.VMEM((STEPS, 4, slots, mc), F32),
            pltpu.VMEM((STEPS, 4, slots, mc), F32),
            pltpu.VMEM((STEPS, 6, slots // 2, mc), BF16),
            pltpu.VMEM((STEPS, 6, slots // 2, mc), BF16),
            pltpu.VMEM((STEPS, ne, 2 * PER, half), BF16),
            pltpu.VMEM((STEPS, ne, 2 * PER, half), BF16),
            pltpu.VMEM((STEPS, NB, SLOTS, mc), F32),
            pltpu.VMEM((STEPS, NB, SLOTS, mc), F32),
            dma((2,)),
            dma,
            dma,
            dma((STEPS, 6)),
            dma((STEPS, 6)),
            dma((STEPS, 11)),
            dma((STEPS, 11)),
            dma((STEPS, 10)),
            dma((STEPS, 10)),
        ],
        compiler_params=pltpu.CompilerParams(
            collective_id=1, has_side_effects=True, vmem_limit_bytes=56 * 2**20
        ),
        cost_estimate=pl.CostEstimate(
            flops=4 * STEPS * slots * d * hs * 2, bytes_accessed=12 * 2**20, transcendentals=0
        ),
        name="layer",
    )(
        source_lengths, parents[:, 0], layer_in[:, 0], queries[:, 0], fresh_entries[:, 0],
        cross_queries[:, 0], jnp.transpose(past_cache[0], (1, 0, 2)), encoder_states[0],
        jnp.transpose(expert_ids[:, 0], (0, 2, 1)), jnp.transpose(gate_weights[:, 0], (0, 2, 1)),
        norm_gain, up_weight, down_weight,
    )
    layer_out, cache_out = pl.pallas_call(
        emit_kernel,
        out_shape=(
            jax.ShapeDtypeStruct((STEPS, SLOTS, d), BF16),
            jax.ShapeDtypeStruct((SLOTS * POS, 2 * d), BF16),
        ),
        in_specs=[vmem, vmem],
        out_specs=(hbm, hbm),
        scratch_shapes=[dma((2,))],
        name="emit",
    )(layer_out, cache_out)
    return layer_out[:, None], cache_out.reshape(1, SLOTS, POS, 2 * d)


def solution(mesh):
    in_specs = (
        P(None, "expert", "batch", None),
        P(None, "expert", "batch", None),
        P(None, "expert", "batch", None),
        P(None, "expert", "batch", None),
        P("expert", "batch", None, None),
        P("expert", "batch", None, None),
        P("expert", "batch"),
        P(None, "expert", None),
        P(None, "expert", None, None),
        P(None, "expert", None, None),
        P(),
        P("expert", None, "batch"),
        P("expert", "batch", None),
    )
    out_specs = (P(None, "expert", "batch", None), P("expert", "batch", None, None))
    return jax.shard_map(shards, mesh=mesh, in_specs=in_specs, out_specs=out_specs, check_vma=False)
```

```python
import functools

import jax
import jax.numpy as jnp
from jax import lax
from jax.experimental import pallas as pl
from jax.experimental.pallas import tpu as pltpu
from jax.sharding import PartitionSpec as P

HEADS = 16
DH = 128
CAP = 4
STEPS = 2
SLOTS = 8
BEAM = 4
CACHE = 14
NB = 8
ROWS = NB * SLOTS
PER = 2 * CAP
POS = 16
MESH = pl.DeviceIdType.MESH
F32 = jnp.float32
BF16 = jnp.bfloat16


def iota(shape, dim):
    return lax.broadcasted_iota(jnp.int32, shape, dim)


def hot(mask):
    return jnp.where(mask, 1.0, 0.0).astype(BF16)


def dot(x, y):
    return jnp.dot(x, y, preferred_element_type=F32)


def move_plan(par):
    n = ROWS
    row, col = iota((n, n), 1), iota((n, n), 0)
    dev_r, dev_c = row // SLOTS, col // SLOTS
    before = jnp.where((row < col) & (dev_r == dev_c), 1.0, 0.0)

    def across(x):
        return jnp.broadcast_to(jnp.sum(x, axis=1, keepdims=True), (n, n))

    def down(x):
        return jnp.broadcast_to(jnp.sum(x, axis=0, keepdims=True), (n, n))

    eye = jnp.where(row == col, 1.0, 0.0)
    par_r = jnp.broadcast_to(par, (n, n))
    takes = jnp.where(col == par_r, 1.0, 0.0)
    cross_r = jnp.where(par_r // SLOTS != dev_r, 1.0, 0.0)
    cross_c = across(eye * cross_r)
    leave_c = across(takes * cross_r)
    leave_r = down(eye * leave_c)
    give_c = across(before * leave_r) + 2.0 * dev_c.astype(F32)
    give_r = down(eye * give_c)
    take_c = across(before * cross_r) + 2.0 * dev_c.astype(F32)
    take_r = down(eye * take_c)
    rowf, colf = row.astype(F32), col.astype(F32)
    given = jnp.where(rowf == give_c, leave_c, 0.0).astype(BF16)
    given_t = jnp.where(colf == give_r, leave_r, 0.0).astype(BF16)
    taken = jnp.where(rowf == take_c, cross_c, 0.0).astype(BF16)
    taken_t = jnp.where(colf == take_r, cross_r, 0.0).astype(BF16)
    takes_t = jnp.transpose(takes).astype(BF16)
    return takes_t, given, given_t, taken, taken_t


def head_mask(rows):
    head = iota((rows, HEADS, HEADS * DH), 1)
    column = iota((rows, HEADS, HEADS * DH), 2) // DH
    return (head == column).astype(F32)


def attend(q, keys, values, valid):
    d = HEADS * DH
    mask = head_mask(SLOTS)
    spread = (jnp.broadcast_to(q[:, None, :], (SLOTS, HEADS, d)) * mask).reshape(SLOTS * HEADS, d)
    scores = lax.dot_general(
        spread.astype(BF16), keys, (((1,), (1,)), ((), ())), preferred_element_type=F32
    ) * (1.0 / DH**0.5)
    scores = jnp.where(valid, scores, -1e30)
    raised = jnp.where(valid, jnp.exp(scores - jnp.max(scores, axis=1, keepdims=True)), 0.0)
    weights = (raised / jnp.sum(raised, axis=1, keepdims=True)).astype(BF16)
    out = jnp.dot(weights, values, preferred_element_type=F32)
    return jnp.sum(out.reshape(SLOTS, HEADS, d) * mask, axis=1)


def layer_kernel(
    ne,
    lens, par, ids, gates, gain, cache_h, fresh_h, cross_h, enc_h, queries_h, layer_h, up_hbm, down_hbm,
    layer_out, cache_out,
    cache, fresh, cross_q, enc, queries, layer_in, wup, wdn, src0, src1, ext1, st_a, pool0, pool1, st_b, cross_s, resid,
    pack_p, gate_hi, gate_lo, hsend, hrecv, psend, xb, hid, sib_s, sib_r, ysend, yrecv,
    rsend, rrecv, fsend, frecv, osem, wsem, lsem, csem, bsend, brecv, agsend, agrecv, sibsend, sibrecv,
):
    b, e = lax.axis_index("batch"), lax.axis_index("expert")
    y, c = b // 2, b % 2
    sib = y * 2 + (1 - c)
    d = HEADS * DH
    kc = 2 * d // NB
    mc = d // NB
    slots = ne * PER
    unsent, unreceived = [], {}
    operands = [
        pltpu.make_async_copy(src, dst, osem.at[k])
        for k, (src, dst) in enumerate(
            (
                (cache_h, cache),
                (fresh_h, fresh),
                (cross_h, cross_q),
                (enc_h, enc),
                (queries_h, queries),
                (layer_h, layer_in),
            )
        )
    ]
    for copy in operands:
        copy.start()

    def peer_y(q):
        return lax.rem(y + q, 4)

    barrier = pltpu.get_barrier_semaphore()

    def greet_b(k, _):
        pl.semaphore_signal(
            barrier, inc=1, device_id=(lax.rem(b + k, NB), e), device_id_type=MESH
        )
        return 0

    def greet_e(k, _):
        pl.semaphore_signal(
            barrier, inc=1, device_id=(b, lax.rem(e + k, ne)), device_id_type=MESH
        )
        return 0

    lax.fori_loop(1, NB, greet_b, 0)
    lax.fori_loop(1, ne, greet_e, 0)

    up_copy = pltpu.make_async_copy(up_hbm, wup, wsem.at[0])
    down_copy = pltpu.make_async_copy(down_hbm, wdn, wsem.at[1])

    def local(src, dst):
        copy = pltpu.make_async_copy(src, dst, lsem)
        copy.start()
        copy.wait()

    def wait_bytes(ref, sem):
        pltpu.make_async_copy(ref, ref, sem).wait()

    def to_all(t, phase, make, ref, axis="batch", span=(1, NB)):
        if span[0] == span[1]:
            unreceived[t, phase] = lambda: None
            return

        def one(k, _):
            src, dst, to = make(k)
            to = (to, e) if axis == "batch" else (b, to)
            pltpu.make_async_remote_copy(
                src, dst, bsend.at[t, phase], brecv.at[t, phase], device_id=to, device_id_type=MESH
            ).start()
            return 0

        lax.fori_loop(span[0], span[1], one, 0)
        unsent.append(lambda: wait_bytes(ref, bsend.at[t, phase]))
        unreceived[t, phase] = lambda: wait_bytes(ref, brecv.at[t, phase])

    mid = ne // 2
    shift = 3 * ne // 4 if ne % 4 == 0 else 0
    own_place = (ne - shift) % ne

    def near_place(i):
        return lax.rem(own_place + i, mid)

    def arrive(t, phase):
        unreceived.pop((t, phase))()

    takes0, given0, given0_t, taken0, taken0_t = move_plan(par[0:1, :])

    near, late = CACHE * SLOTS, CACHE * SLOTS + 2 * POS
    operands[0].wait()
    src0[0:near] = cache[...].astype(F32).reshape(near, 2 * d).astype(BF16)

    same_dev = iota((ROWS, ROWS), 0) // SLOTS == iota((ROWS, ROWS), 1) // SLOTS
    own_m = hot(iota((2 * POS, ROWS), 1) == 2 * b + iota((2 * POS, ROWS), 0) // POS)
    near_c = hot(iota((ROWS, near), 0) == SLOTS * b + iota((ROWS, near), 1) % SLOTS)
    near_p = iota((2 * POS, near), 0) % POS == iota((2 * POS, near), 1) // SLOTS

    def given_rows(chosen):
        pick = dot(dot(own_m, chosen).astype(BF16), near_c)
        return dot(jnp.where(near_p, pick, 0.0).astype(BF16), src0[0:near])

    st_a[0] = given_rows(given0_t).astype(BF16)

    pl.semaphore_wait(barrier, NB - 1 + ne - 1)

    pools = (pool0, pool1)

    def own_cols(k):
        return pl.ds(pl.multiple_of(k * kc, kc), kc)

    def own_rows(k):
        return pl.ds(pl.multiple_of(k * 2 * POS, 2 * POS), 2 * POS)

    def send_a(t):
        def make(k):
            to = lax.rem(b + k, NB)
            return st_a.at[t, :, own_cols(to)], pools[t].at[own_rows(b)], to

        to_all(t, 0, make, st_b.at[t, pl.ds(0, 14 * POS)])
        local(st_a.at[t, :, own_cols(b)], pools[t].at[own_rows(b)])

    def send_b(t):
        landing = src0.at[near:late] if t == 0 else src1.at[SLOTS * POS : SLOTS * POS + 2 * POS]

        def make(k):
            to = lax.rem(b + k, NB)
            return st_b.at[t, own_rows(to)], landing.at[:, own_cols(b)], to

        to_all(t, 1, make, st_b.at[t, pl.ds(0, 14 * POS)])
        local(st_b.at[t, own_rows(b)], landing.at[:, own_cols(b)])

    send_a(0)
    up_copy.start()
    down_copy.start()
    operands[1].wait()
    blank = jnp.zeros((SLOTS, 2 * d), F32)
    src0[late:] = jnp.concatenate([fresh[0].astype(F32), blank], axis=0).astype(BF16)
    src1[late + POS :] = jnp.concatenate([fresh[1].astype(F32), blank], axis=0).astype(BF16)

    takes1, given1, given1_t, taken1, taken1_t = move_plan(par[1:2, :])
    kept1_t = dot(given1_t, jnp.where(same_dev, takes0.astype(F32), 0.0).astype(BF16)).astype(BF16)
    slot_c = hot(
        (iota((ROWS, POS), 0) == SLOTS * b + iota((ROWS, POS), 1)) & (iota((ROWS, POS), 1) < SLOTS)
    )
    entry = dot(dot(own_m, given1_t).astype(BF16), slot_c)
    entry = jnp.where(iota((2 * POS, POS), 0) % POS == CACHE, entry, 0.0).astype(BF16)
    st_a[1] = (given_rows(kept1_t) + dot(entry, src0[late:])).astype(BF16)

    own_s = iota((SLOTS * HEADS, 64), 0) // (HEADS * BEAM)
    key_i = iota((SLOTS * HEADS, 64), 1)
    limit = jnp.where(own_s == 0, lens[0, 0], lens[0, 1])
    cross_valid = (key_i // 32 == own_s) & (key_i % 32 < limit)

    def cross(t):
        enc_k = enc[:, :, :d].reshape(64, d)
        enc_v = enc[:, :, d:].reshape(64, d)
        cross_s[t] = attend(cross_q[t].astype(F32), enc_k, enc_v, cross_valid)

    def route(t):
        slot = iota((slots, ROWS), 0)
        owner = lax.rem(slot // PER + shift + e, ne)
        expert = owner * 2 + slot % PER // CAP
        earlier = hot(iota((ROWS, ROWS), 0) < iota((ROWS, ROWS), 1))
        first = jnp.where(ids[t, 0:1, :] == expert, 1.0, 0.0)
        second = jnp.where(ids[t, 1:2, :] == expert, 1.0, 0.0)
        named = first + second
        rank = dot(named.astype(BF16), earlier)
        chosen = jnp.where(rank == (slot % CAP).astype(F32), named, 0.0)
        pack_p[t] = chosen.astype(BF16)
        weight = chosen * (first * gates[t, 0:1, :] + second * gates[t, 1:2, :])
        weight = jnp.transpose(weight)
        high = weight.astype(BF16)
        gate_hi[t] = high
        gate_lo[t] = (weight - high.astype(F32)).astype(BF16)

    pairs = 2 * NB * POS
    pair_m = hot(iota((pairs, ROWS), 0) // POS == iota((pairs, ROWS), 1))
    pair_mt = hot(iota((ROWS, pairs), 0) == iota((ROWS, pairs), 1) // POS)
    same_p = iota((pairs, pairs), 0) % POS == iota((pairs, pairs), 1) % POS

    def spread(small):
        wide = dot(dot(pair_m, small.astype(BF16)).astype(BF16), pair_mt)
        return jnp.where(same_p, wide, 0.0).astype(BF16)

    from0 = dot(takes0, given0).astype(BF16)
    hand0 = spread(dot(taken0_t, from0))

    def select(t, takes, taken):
        held = near if t == 0 else SLOTS * POS
        width = held + 2 * POS + POS
        shape = (SLOTS * POS, width)
        k, out_p, out_r = iota(shape, 1), iota(shape, 0) % POS, iota(shape, 0) // POS
        own_r = hot(
            iota((SLOTS * POS, ROWS), 1) == SLOTS * b + iota((SLOTS * POS, ROWS), 0) // POS
        )
        kk, cc = iota((ROWS, width), 1), iota((ROWS, width), 0)
        slot = kk % SLOTS if t == 0 else kk // POS
        at_c = hot((kk < held) & (cc == SLOTS * b + slot))
        at_m = hot((kk >= held) & (kk < held + 2 * POS) & (cc == 2 * b + (kk - held) // POS))
        picked = dot(dot(own_r, takes).astype(BF16), at_c)
        picked = picked + dot(dot(own_r, taken).astype(BF16), at_m)
        old_p = k // SLOTS if t == 0 else k % POS
        key_p = jnp.where(k < held, old_p, (k - held) % POS)
        picked = jnp.where((key_p == out_p) & (k < held + 2 * POS), picked, 0.0)
        new = (k - (held + 2 * POS) == out_r) & (out_p == CACHE + t)
        return jnp.where(new, 1.0, picked).astype(BF16)

    via1 = dot(taken1_t, takes1).astype(BF16)
    arrive(0, 0)
    st_b[0] = dot(hand0, pool0[...]).astype(BF16)
    send_b(0)
    send_a(1)
    hand1_old = spread(dot(via1, from0))
    hand1_new = spread(dot(via1, given1))
    select0 = select(0, takes0, taken0)
    for copy in operands[2:]:
        copy.wait()
    cross(0)

    own_r = iota((SLOTS * HEADS, SLOTS * POS), 0) // HEADS
    self_key = iota((SLOTS * HEADS, SLOTS * POS), 1)

    def attention(t):
        arrive(t, 1)
        if t == 0:
            src1[0 : SLOTS * POS] = dot(select0, src0[...]).astype(BF16)
            held = src1
        else:
            ext1[...] = dot(select1, src1[...]).astype(BF16)
            held = ext1
            pltpu.make_async_copy(ext1, cache_out, csem).start()
            unsent.append(lambda: pltpu.make_async_copy(ext1, cache_out, csem).wait())
        valid = (self_key // POS == own_r) & (self_key % POS < CACHE + 1 + t)
        keys = held[0 : SLOTS * POS, :d]
        values = held[0 : SLOTS * POS, d:]
        state = (
            layer_in[t].astype(F32)
            + attend(queries[t].astype(F32), keys, values, valid)
            + cross_s[t]
        )
        resid[t] = state
        centered = state - jnp.mean(state, axis=1, keepdims=True)
        variance = jnp.mean(centered * centered, axis=1, keepdims=True)
        gains = gain[...].astype(F32).reshape(1, d)
        normed = centered * lax.rsqrt(variance + 1e-05) * gains
        for j in range(NB):
            hsend[t, j] = normed[:, j * mc : (j + 1) * mc]

        def make(k):
            to = lax.rem(b + k, NB)
            return hsend.at[t, to], hrecv.at[t, b], to

        to_all(t, 2, make, hsend.at[t, pl.ds(0, NB - 1)])
        hrecv[t, b] = hsend[t, b]

    half = mc // 2

    def halves(x):
        n = x.shape[0] // PER
        left = x[:, :half].reshape(n, PER, half)
        right = x[:, half:].reshape(n, PER, half)
        return jnp.concatenate([left, right], axis=1).astype(BF16)

    def whole(x):
        x = x.astype(F32)
        left = x[:, :PER].reshape(slots, half)
        right = x[:, PER:].reshape(slots, half)
        return jnp.concatenate([left, right], axis=1).astype(BF16)

    def dispatch(t):
        arrive(t, 2)
        rows = hrecv[t].reshape(ROWS, mc).astype(BF16)
        psend[t] = halves(dot(pack_p[t], rows))

        def make(s):
            return psend.at[t, s], xb.at[t, b, s], lax.rem(e + s + shift, ne)

        to_all(
            t, 3, lambda i: make(near_place(i)), psend.at[t, pl.ds(0, mid - 1)], "expert", (1, mid)
        )
        to_all(t, 6, make, psend.at[t, pl.ds(0, mid)], "expert", (mid, ne))
        xb[t, b, own_place] = psend[t, own_place]

    low, high = pl.ds(0, ne // 2), pl.ds(ne // 2, ne // 2)
    every = pl.ds(0, ne)
    up_y, down_y = peer_y(1) * 2, peer_y(3) * 2
    far_y = peer_y(2) * 2

    def ag_copy(t, which):
        block, part, to = (
            (b, every, sib),
            (b, low, up_y + c),
            (b, high, down_y + c),
            (b, high, up_y + c),
            (b, low, down_y + c),
            (down_y + c, low, up_y + c),
            (up_y + c, high, down_y + c),
            (down_y + c, every, sib),
            (up_y + c, every, sib),
            (far_y + c, low, sib),
            (far_y + c, high, sib),
        )[which]
        return pltpu.make_async_remote_copy(
            xb.at[t, block, part], xb.at[t, block, part],
            agsend.at[t, which], agrecv.at[t, which], device_id=(to, e), device_id_type=MESH,
        )

    def gather_start(t):
        arrive(t, 3)
        for which in (1, 4):
            ag_copy(t, which).start()
        arrive(t, 6)
        for which in (2, 3, 0):
            ag_copy(t, which).start()
        for which in range(11):
            unsent.append(lambda which=which: ag_copy(t, which).wait_send())

    def gather_relay(t, stage):
        if stage == 0:
            for came, relay in ((1, 5), (2, 6)):
                ag_copy(t, came).wait_recv()
                ag_copy(t, relay).start()
        else:
            for came, pass_on in ((3, 7), (4, 8)):
                ag_copy(t, came).wait_recv()
                ag_copy(t, pass_on).start()

    def up_part(t, block, first):
        x = whole(xb[t, block])
        at = pl.ds(pl.multiple_of(block * mc, mc), mc)
        for k in range(2):
            part = jnp.dot(x, wup[k, at, :], preferred_element_type=F32)
            if first:
                hid[k] = part
            else:
                hid[k] += part

    def gather_compute(t):
        up_part(t, b, True)
        ag_copy(t, 0).wait_recv()
        up_part(t, sib, False)
        up_part(t, down_y + c, False)
        up_part(t, up_y + c, False)
        for came, pass_on in ((5, 9), (6, 10)):
            ag_copy(t, came).wait_recv()
            ag_copy(t, pass_on).start()
        ag_copy(t, 7).wait_recv()
        up_part(t, down_y + 1 - c, False)
        ag_copy(t, 8).wait_recv()
        up_part(t, up_y + 1 - c, False)
        up_part(t, far_y + c, False)
        ag_copy(t, 9).wait_recv()
        ag_copy(t, 10).wait_recv()
        up_part(t, far_y + 1 - c, False)

    def down_part(t, block, acts):
        at = pl.ds(pl.multiple_of(block * mc, mc), mc)
        return jnp.dot(acts[0], wdn[0, :, at], preferred_element_type=F32) + jnp.dot(
            acts[1], wdn[1, :, at], preferred_element_type=F32
        )

    def sib_copy(t, q):
        return pltpu.make_async_remote_copy(
            sib_s.at[t, q], sib_r.at[t, q],
            sibsend.at[t, q], sibrecv.at[t, q], device_id=(sib, e), device_id_type=MESH,
        )

    def y_copy(t, which):
        to = (up_y, down_y, up_y, down_y, up_y, down_y)[which] + c
        return pltpu.make_async_remote_copy(
            ysend.at[t, which], yrecv.at[t, which],
            sibsend.at[t, 4 + which], sibrecv.at[t, 4 + which],
            device_id=(to, e), device_id_type=MESH,
        )

    first, second = slice(0, slots // 2), slice(slots // 2, slots)

    def y_send(t, which, part):
        ysend[t, which] = part.astype(BF16)
        y_copy(t, which).start()

    def scatter_start(t, between):
        for q in range(4):
            unsent.append(lambda q=q: sib_copy(t, q).wait_send())
        for which in range(6):
            unsent.append(lambda which=which: y_copy(t, which).wait_send())
        own = iota((slots, hid.shape[2]), 0) % PER // CAP
        acts = [
            jnp.where(own == k, jnp.maximum(hid[k], 0.0), 0.0).astype(BF16) for k in range(2)
        ]
        def for_sib(q):
            sib_s[t, q] = down_part(t, peer_y(q) * 2 + (1 - c), acts)
            sib_copy(t, q).start()

        for_sib(2)
        for q, after in ((2, 1), (1, 3), (3, 0), (0, None)):
            if after is not None:
                for_sib(after)
            if q == 3:
                between()
            part = down_part(t, peer_y(q) * 2 + c, acts)
            sib_copy(t, q).wait_recv()
            part = part + sib_r[t, q]
            if q == 2:
                y_send(t, 0, part[first])
                y_send(t, 1, part[second])
            elif q == 1:
                y_send(t, 2, part[second])
                sib_r[t, 1, first] = part[first]
            elif q == 3:
                y_send(t, 3, part[first])
                sib_r[t, 3, second] = part[second]
            else:
                sib_r[t, 0] = part

    def scatter_relay(t):
        y_copy(t, 0).wait_recv()
        y_send(t, 4, sib_r[t, 1, first] + yrecv[t, 0].astype(F32))
        y_copy(t, 1).wait_recv()
        y_send(t, 5, sib_r[t, 3, second] + yrecv[t, 1].astype(F32))

    def give_back(t):
        def make(s):
            return rsend.at[t, s], rrecv.at[t, s], lax.rem(e - s - shift + 2 * ne, ne)

        for which in (2, 5):
            y_copy(t, which).wait_recv()
        total = sib_r[t, 0, second] + yrecv[t, 2].astype(F32) + yrecv[t, 5].astype(F32)
        rsend[t, mid:] = halves(total)
        to_all(t, 7, make, rsend.at[t, pl.ds(0, mid)], "expert", (mid, ne))
        for which in (3, 4):
            y_copy(t, which).wait_recv()
        total = sib_r[t, 0, first] + yrecv[t, 3].astype(F32) + yrecv[t, 4].astype(F32)
        rsend[t, :mid] = halves(total)
        to_all(
            t, 4, lambda i: make(near_place(i)), rsend.at[t, pl.ds(0, mid - 1)], "expert", (1, mid)
        )
        rrecv[t, own_place] = rsend[t, own_place]

    def combine(t):
        arrive(t, 7)
        arrive(t, 4)
        came = whole(rrecv[t])
        mixed = jnp.dot(gate_hi[t], came, preferred_element_type=F32) + jnp.dot(
            gate_lo[t], came, preferred_element_type=F32
        )
        fsend[t] = mixed.reshape(NB, SLOTS, mc)

        def make(k):
            to = lax.rem(b + k, NB)
            return fsend.at[t, to], frecv.at[t, b], to

        to_all(t, 5, make, fsend.at[t, pl.ds(0, NB - 1)])
        frecv[t, b] = fsend[t, b]

    def finish(t):
        arrive(t, 5)
        for j in range(NB):
            cols = slice(j * mc, (j + 1) * mc)
            layer_out[t, :, cols] = (resid[t, :, cols] + frecv[t, j]).astype(BF16)

    attention(0)
    arrive(1, 0)
    st_b[1] = (dot(hand1_old, pool0[...]) + dot(hand1_new, pool1[...])).astype(BF16)
    send_b(1)
    route(0)
    dispatch(0)
    select1 = select(1, takes1, taken1)
    cross(1)
    attention(1)
    route(1)
    gather_start(0)
    dispatch(1)
    up_copy.wait()
    gather_relay(0, 0)
    gather_relay(0, 1)
    gather_start(1)
    gather_compute(0)
    down_copy.wait()
    gather_relay(1, 0)
    scatter_start(0, lambda: gather_relay(1, 1))
    gather_compute(1)
    scatter_relay(0)
    scatter_start(1, lambda: None)
    give_back(0)
    scatter_relay(1)
    give_back(1)
    combine(0)
    finish(0)
    combine(1)
    finish(1)

    for done in unsent:
        done()


def emit_kernel(layer_in, cache_in, layer_out, cache_out, sem):
    copies = [
        pltpu.make_async_copy(cache_in, cache_out, sem.at[0]),
        pltpu.make_async_copy(layer_in, layer_out, sem.at[1]),
    ]
    for copy in copies:
        copy.start()
    for copy in copies:
        copy.wait()


def shards(
    layer_in, queries, fresh_entries, cross_queries, past_cache, encoder_states, source_lengths,
    parents, expert_ids, gate_weights, norm_gain, up_weight, down_weight,
):
    ne = lax.axis_size("expert")
    d = HEADS * DH
    mc = d // NB
    half = mc // 2
    kc = 2 * d // NB
    slots = ne * PER
    hs = up_weight.shape[2]
    vmem = pl.BlockSpec(memory_space=pltpu.VMEM)
    smem = pl.BlockSpec(memory_space=pltpu.SMEM)
    hbm = pl.BlockSpec(memory_space=pl.ANY)
    dma = pltpu.SemaphoreType.DMA
    layer_out, cache_out = pl.pallas_call(
        functools.partial(layer_kernel, ne),
        out_shape=(
            jax.ShapeDtypeStruct((STEPS, SLOTS, d), BF16),
            jax.ShapeDtypeStruct((SLOTS * POS, 2 * d), BF16),
        ),
        in_specs=[smem] + [vmem] * 4 + [hbm] * 8,
        out_specs=(vmem, hbm),
        scratch_shapes=[
            pltpu.VMEM((CACHE, SLOTS, 2 * d), BF16),
            pltpu.VMEM((STEPS, SLOTS, 2 * d), BF16),
            pltpu.VMEM((STEPS, SLOTS, d), BF16),
            pltpu.VMEM((2, 32, 2 * d), BF16),
            pltpu.VMEM((STEPS, SLOTS, d), BF16),
            pltpu.VMEM((STEPS, SLOTS, d), BF16),
            pltpu.VMEM((2, d, hs), BF16),
            pltpu.VMEM((2, hs, d), BF16),
            pltpu.VMEM((CACHE * SLOTS + 2 * POS + POS, 2 * d), BF16),
            pltpu.VMEM((SLOTS * POS + 2 * POS + POS, 2 * d), BF16),
            pltpu.VMEM((SLOTS * POS, 2 * d), BF16),
            pltpu.VMEM((STEPS, 2 * POS, 2 * d), BF16),
            pltpu.VMEM((2 * NB * POS, kc), BF16),
            pltpu.VMEM((2 * NB * POS, kc), BF16),
            pltpu.VMEM((STEPS, 2 * NB * POS, kc), BF16),
            pltpu.VMEM((STEPS, SLOTS, d), F32),
            pltpu.VMEM((STEPS, SLOTS, d), F32),
            pltpu.VMEM((STEPS, slots, ROWS), BF16),
            pltpu.VMEM((STEPS, ROWS, slots), BF16),
            pltpu.VMEM((STEPS, ROWS, slots), BF16),
            pltpu.VMEM((STEPS, NB, SLOTS, mc), F32),
            pltpu.VMEM((STEPS, NB, SLOTS, mc), F32),
            pltpu.VMEM((STEPS, ne, 2 * PER, half), BF16),
            pltpu.VMEM((STEPS, NB, ne, 2 * PER, half), BF16),
            pltpu.VMEM((2, slots, hs), F32),
            pltpu.VMEM((STEPS, 4, slots, mc), F32),
            pltpu.VMEM((STEPS, 4, slots, mc), F32),
            pltpu.VMEM((STEPS, 6, slots // 2, mc), BF16),
            pltpu.VMEM((STEPS, 6, slots // 2, mc), BF16),
            pltpu.VMEM((STEPS, ne, 2 * PER, half), BF16),
            pltpu.VMEM((STEPS, ne, 2 * PER, half), BF16),
            pltpu.VMEM((STEPS, NB, SLOTS, mc), F32),
            pltpu.VMEM((STEPS, NB, SLOTS, mc), F32),
            dma((6,)),
            dma((2,)),
            dma,
            dma,
            dma((STEPS, 8)),
            dma((STEPS, 8)),
            dma((STEPS, 11)),
            dma((STEPS, 11)),
            dma((STEPS, 10)),
            dma((STEPS, 10)),
        ],
        compiler_params=pltpu.CompilerParams(
            collective_id=1, has_side_effects=True, vmem_limit_bytes=56 * 2**20
        ),
        cost_estimate=pl.CostEstimate(
            flops=4 * STEPS * slots * d * hs * 2, bytes_accessed=12 * 2**20, transcendentals=0
        ),
        name="layer",
    )(
        source_lengths, parents[:, 0], jnp.transpose(expert_ids[:, 0], (0, 2, 1)),
        jnp.transpose(gate_weights[:, 0], (0, 2, 1)), norm_gain,
        jnp.transpose(past_cache[0], (1, 0, 2)), fresh_entries[:, 0], cross_queries[:, 0],
        encoder_states[0], queries[:, 0], layer_in[:, 0], up_weight, down_weight,
    )
    layer_out, cache_out = pl.pallas_call(
        emit_kernel,
        out_shape=(
            jax.ShapeDtypeStruct((STEPS, SLOTS, d), BF16),
            jax.ShapeDtypeStruct((SLOTS * POS, 2 * d), BF16),
        ),
        in_specs=[vmem, vmem],
        out_specs=(hbm, hbm),
        scratch_shapes=[dma((2,))],
        name="emit",
    )(layer_out, cache_out)
    return layer_out[:, None], cache_out.reshape(1, SLOTS, POS, 2 * d)


def solution(mesh):
    in_specs = (
        P(None, "expert", "batch", None),
        P(None, "expert", "batch", None),
        P(None, "expert", "batch", None),
        P(None, "expert", "batch", None),
        P("expert", "batch", None, None),
        P("expert", "batch", None, None),
        P("expert", "batch"),
        P(None, "expert", None),
        P(None, "expert", None, None),
        P(None, "expert", None, None),
        P(),
        P("expert", None, "batch"),
        P("expert", "batch", None),
    )
    out_specs = (P(None, "expert", "batch", None), P("expert", "batch", None, None))
    return jax.shard_map(shards, mesh=mesh, in_specs=in_specs, out_specs=out_specs, check_vma=False)
```

```python
import functools

import jax
import jax.numpy as jnp
from jax import lax
from jax.experimental import pallas as pl
from jax.experimental.pallas import tpu as pltpu
from jax.sharding import PartitionSpec as P

HEADS = 16
DH = 128
CAP = 4
STEPS = 2
SLOTS = 8
BEAM = 4
CACHE = 14
NB = 8
ROWS = NB * SLOTS
PER = 2 * CAP
POS = 16
MESH = pl.DeviceIdType.MESH
F32 = jnp.float32
BF16 = jnp.bfloat16


def iota(shape, dim):
    return lax.broadcasted_iota(jnp.int32, shape, dim)


def hot(mask):
    return jnp.where(mask, 1.0, 0.0).astype(BF16)


def dot(x, y):
    return jnp.dot(x, y, preferred_element_type=F32)


def move_plan(par):
    n = ROWS
    row, col = iota((n, n), 1), iota((n, n), 0)
    dev_r, dev_c = row // SLOTS, col // SLOTS
    before = jnp.where((row < col) & (dev_r == dev_c), 1.0, 0.0)

    def across(x):
        return jnp.broadcast_to(jnp.sum(x, axis=1, keepdims=True), (n, n))

    def down(x):
        return jnp.broadcast_to(jnp.sum(x, axis=0, keepdims=True), (n, n))

    eye = jnp.where(row == col, 1.0, 0.0)
    par_r = jnp.broadcast_to(par, (n, n))
    takes = jnp.where(col == par_r, 1.0, 0.0)
    cross_r = jnp.where(par_r // SLOTS != dev_r, 1.0, 0.0)
    cross_c = across(eye * cross_r)
    leave_c = across(takes * cross_r)
    leave_r = down(eye * leave_c)
    give_c = across(before * leave_r) + 2.0 * dev_c.astype(F32)
    give_r = down(eye * give_c)
    take_c = across(before * cross_r) + 2.0 * dev_c.astype(F32)
    take_r = down(eye * take_c)
    rowf, colf = row.astype(F32), col.astype(F32)
    given = jnp.where(rowf == give_c, leave_c, 0.0).astype(BF16)
    given_t = jnp.where(colf == give_r, leave_r, 0.0).astype(BF16)
    taken = jnp.where(rowf == take_c, cross_c, 0.0).astype(BF16)
    taken_t = jnp.where(colf == take_r, cross_r, 0.0).astype(BF16)
    takes_t = jnp.transpose(takes).astype(BF16)
    return takes_t, given, given_t, taken, taken_t


def head_mask(rows):
    head = iota((rows, HEADS, HEADS * DH), 1)
    column = iota((rows, HEADS, HEADS * DH), 2) // DH
    return (head == column).astype(F32)


def attend(q, keys, values, valid):
    d = HEADS * DH
    mask = head_mask(SLOTS)
    spread = (jnp.broadcast_to(q[:, None, :], (SLOTS, HEADS, d)) * mask).reshape(SLOTS * HEADS, d)
    scores = lax.dot_general(
        spread.astype(BF16), keys, (((1,), (1,)), ((), ())), preferred_element_type=F32
    ) * (1.0 / DH**0.5)
    scores = jnp.where(valid, scores, -1e30)
    raised = jnp.where(valid, jnp.exp(scores - jnp.max(scores, axis=1, keepdims=True)), 0.0)
    weights = (raised / jnp.sum(raised, axis=1, keepdims=True)).astype(BF16)
    out = jnp.dot(weights, values, preferred_element_type=F32)
    return jnp.sum(out.reshape(SLOTS, HEADS, d) * mask, axis=1)


def layer_kernel(
    ne,
    lens, par, ids, gates, gain, cache_h, fresh_h, cross_h, enc_h, queries_h, layer_h, up_hbm, down_hbm,
    layer_out, cache_out,
    cache, fresh, cross_q, enc, queries, layer_in, wup, wdn, src0, src1, ext1, st_a, pool0, pool1, st_b, cross_s, resid,
    pack_p, gate_hi, gate_lo, hsend, hrecv, psend, xb, hid, sib_s, sib_r, ysend, yrecv,
    rsend, rrecv, fsend, frecv, osem, wsem, lsem, csem, bsend, brecv, agsend, agrecv, sibsend, sibrecv,
):
    b, e = lax.axis_index("batch"), lax.axis_index("expert")
    y, c = b // 2, b % 2
    sib = y * 2 + (1 - c)
    d = HEADS * DH
    kc = 2 * d // NB
    mc = d // NB
    slots = ne * PER
    unsent, unreceived = [], {}
    operands = [
        pltpu.make_async_copy(src, dst, osem.at[k])
        for k, (src, dst) in enumerate(
            (
                (cache_h, cache),
                (fresh_h, fresh),
                (cross_h, cross_q),
                (enc_h, enc),
                (queries_h, queries),
                (layer_h, layer_in),
            )
        )
    ]
    for copy in operands:
        copy.start()

    def peer_y(q):
        return lax.rem(y + q, 4)

    barrier = pltpu.get_barrier_semaphore()

    def greet_b(k, _):
        pl.semaphore_signal(
            barrier, inc=1, device_id=(lax.rem(b + k, NB), e), device_id_type=MESH
        )
        return 0

    def greet_e(k, _):
        pl.semaphore_signal(
            barrier, inc=1, device_id=(b, lax.rem(e + k, ne)), device_id_type=MESH
        )
        return 0

    lax.fori_loop(1, NB, greet_b, 0)
    lax.fori_loop(1, ne, greet_e, 0)

    up_copy = pltpu.make_async_copy(up_hbm, wup, wsem.at[0])
    down_copy = pltpu.make_async_copy(down_hbm, wdn, wsem.at[1])

    def local(t, phase, src, dst):
        copy = pltpu.make_async_copy(src, dst, lsem.at[t, phase])
        copy.start()
        others = unreceived[t, phase]

        def both():
            others()
            copy.wait()

        unreceived[t, phase] = both

    def wait_bytes(ref, sem):
        pltpu.make_async_copy(ref, ref, sem).wait()

    def to_all(t, phase, make, ref, axis="batch", span=(1, NB)):
        if span[0] == span[1]:
            unreceived[t, phase] = lambda: None
            return

        def one(k, _):
            src, dst, to = make(k)
            to = (to, e) if axis == "batch" else (b, to)
            pltpu.make_async_remote_copy(
                src, dst, bsend.at[t, phase], brecv.at[t, phase], device_id=to, device_id_type=MESH
            ).start()
            return 0

        lax.fori_loop(span[0], span[1], one, 0)
        unsent.append(lambda: wait_bytes(ref, bsend.at[t, phase]))
        unreceived[t, phase] = lambda: wait_bytes(ref, brecv.at[t, phase])

    mid = ne // 2
    shift = 3 * ne // 4 if ne % 4 == 0 else 0
    own_place = (ne - shift) % ne

    def near_place(i):
        return lax.rem(own_place + i, mid)

    def arrive(t, phase):
        unreceived.pop((t, phase))()

    takes0, given0, given0_t, taken0, taken0_t = move_plan(par[0:1, :])

    near, late = CACHE * SLOTS, CACHE * SLOTS + 2 * POS
    operands[0].wait()
    src0[0:near] = cache[...].astype(F32).reshape(near, 2 * d).astype(BF16)

    same_dev = iota((ROWS, ROWS), 0) // SLOTS == iota((ROWS, ROWS), 1) // SLOTS
    own_m = hot(iota((2 * POS, ROWS), 1) == 2 * b + iota((2 * POS, ROWS), 0) // POS)
    near_c = hot(iota((ROWS, near), 0) == SLOTS * b + iota((ROWS, near), 1) % SLOTS)
    near_p = iota((2 * POS, near), 0) % POS == iota((2 * POS, near), 1) // SLOTS

    def given_rows(chosen):
        pick = dot(dot(own_m, chosen).astype(BF16), near_c)
        return dot(jnp.where(near_p, pick, 0.0).astype(BF16), src0[0:near])

    st_a[0] = given_rows(given0_t).astype(BF16)

    pl.semaphore_wait(barrier, NB - 1 + ne - 1)

    pools = (pool0, pool1)

    def own_cols(k):
        return pl.ds(pl.multiple_of(k * kc, kc), kc)

    def own_rows(k):
        return pl.ds(pl.multiple_of(k * 2 * POS, 2 * POS), 2 * POS)

    def send_a(t):
        def make(k):
            to = lax.rem(b + k, NB)
            return st_a.at[t, :, own_cols(to)], pools[t].at[own_rows(b)], to

        to_all(t, 0, make, st_b.at[t, pl.ds(0, 14 * POS)])
        local(t, 0, st_a.at[t, :, own_cols(b)], pools[t].at[own_rows(b)])

    def send_b(t):
        landing = src0.at[near:late] if t == 0 else src1.at[SLOTS * POS : SLOTS * POS + 2 * POS]

        def make(k):
            to = lax.rem(b + k, NB)
            return st_b.at[t, own_rows(to)], landing.at[:, own_cols(b)], to

        to_all(t, 1, make, st_b.at[t, pl.ds(0, 14 * POS)])
        local(t, 1, st_b.at[t, own_rows(b)], landing.at[:, own_cols(b)])

    send_a(0)
    up_copy.start()
    down_copy.start()
    operands[1].wait()
    blank = jnp.zeros((SLOTS, 2 * d), F32)
    src0[late:] = jnp.concatenate([fresh[0].astype(F32), blank], axis=0).astype(BF16)
    src1[late + POS :] = jnp.concatenate([fresh[1].astype(F32), blank], axis=0).astype(BF16)

    takes1, given1, given1_t, taken1, taken1_t = move_plan(par[1:2, :])
    kept1_t = dot(given1_t, jnp.where(same_dev, takes0.astype(F32), 0.0).astype(BF16)).astype(BF16)
    slot_c = hot(
        (iota((ROWS, POS), 0) == SLOTS * b + iota((ROWS, POS), 1)) & (iota((ROWS, POS), 1) < SLOTS)
    )
    entry = dot(dot(own_m, given1_t).astype(BF16), slot_c)
    entry = jnp.where(iota((2 * POS, POS), 0) % POS == CACHE, entry, 0.0).astype(BF16)
    st_a[1] = (given_rows(kept1_t) + dot(entry, src0[late:])).astype(BF16)
    send_a(1)

    own_s = iota((SLOTS * HEADS, 64), 0) // (HEADS * BEAM)
    key_i = iota((SLOTS * HEADS, 64), 1)
    limit = jnp.where(own_s == 0, lens[0, 0], lens[0, 1])
    cross_valid = (key_i // 32 == own_s) & (key_i % 32 < limit)

    def cross(t):
        enc_k = enc[:, :, :d].reshape(64, d)
        enc_v = enc[:, :, d:].reshape(64, d)
        cross_s[t] = attend(cross_q[t].astype(F32), enc_k, enc_v, cross_valid)

    def route(t):
        slot = iota((slots, ROWS), 0)
        owner = lax.rem(slot // PER + shift + e, ne)
        expert = owner * 2 + slot % PER // CAP
        earlier = hot(iota((ROWS, ROWS), 0) < iota((ROWS, ROWS), 1))
        first = jnp.where(ids[t, 0:1, :] == expert, 1.0, 0.0)
        second = jnp.where(ids[t, 1:2, :] == expert, 1.0, 0.0)
        named = first + second
        rank = dot(named.astype(BF16), earlier)
        chosen = jnp.where(rank == (slot % CAP).astype(F32), named, 0.0)
        pack_p[t] = chosen.astype(BF16)
        weight = chosen * (first * gates[t, 0:1, :] + second * gates[t, 1:2, :])
        weight = jnp.transpose(weight)
        high = weight.astype(BF16)
        gate_hi[t] = high
        gate_lo[t] = (weight - high.astype(F32)).astype(BF16)

    pairs = 2 * NB * POS
    pair_m = hot(iota((pairs, ROWS), 0) // POS == iota((pairs, ROWS), 1))
    pair_mt = hot(iota((ROWS, pairs), 0) == iota((ROWS, pairs), 1) // POS)
    same_p = iota((pairs, pairs), 0) % POS == iota((pairs, pairs), 1) % POS

    def spread(small):
        wide = dot(dot(pair_m, small.astype(BF16)).astype(BF16), pair_mt)
        return jnp.where(same_p, wide, 0.0).astype(BF16)

    from0 = dot(takes0, given0).astype(BF16)
    hand0 = spread(dot(taken0_t, from0))

    def select(t, takes, taken):
        held = near if t == 0 else SLOTS * POS
        width = held + 2 * POS + POS
        shape = (SLOTS * POS, width)
        k, out_p, out_r = iota(shape, 1), iota(shape, 0) % POS, iota(shape, 0) // POS
        own_r = hot(
            iota((SLOTS * POS, ROWS), 1) == SLOTS * b + iota((SLOTS * POS, ROWS), 0) // POS
        )
        kk, cc = iota((ROWS, width), 1), iota((ROWS, width), 0)
        slot = kk % SLOTS if t == 0 else kk // POS
        at_c = hot((kk < held) & (cc == SLOTS * b + slot))
        at_m = hot((kk >= held) & (kk < held + 2 * POS) & (cc == 2 * b + (kk - held) // POS))
        picked = dot(dot(own_r, takes).astype(BF16), at_c)
        picked = picked + dot(dot(own_r, taken).astype(BF16), at_m)
        old_p = k // SLOTS if t == 0 else k % POS
        key_p = jnp.where(k < held, old_p, (k - held) % POS)
        picked = jnp.where((key_p == out_p) & (k < held + 2 * POS), picked, 0.0)
        new = (k - (held + 2 * POS) == out_r) & (out_p == CACHE + t)
        return jnp.where(new, 1.0, picked).astype(BF16)

    via1 = dot(taken1_t, takes1).astype(BF16)
    arrive(0, 0)
    st_b[0] = dot(hand0, pool0[...]).astype(BF16)
    send_b(0)
    hand1_old = spread(dot(via1, from0))
    hand1_new = spread(dot(via1, given1))
    select0 = select(0, takes0, taken0)
    for copy in operands[2:]:
        copy.wait()
    cross(0)
    arrive(1, 0)
    st_b[1] = (dot(hand1_old, pool0[...]) + dot(hand1_new, pool1[...])).astype(BF16)
    send_b(1)

    own_r = iota((SLOTS * HEADS, SLOTS * POS), 0) // HEADS
    self_key = iota((SLOTS * HEADS, SLOTS * POS), 1)

    def attention(t):
        arrive(t, 1)
        if t == 0:
            src1[0 : SLOTS * POS] = dot(select0, src0[...]).astype(BF16)
            held = src1
        else:
            ext1[...] = dot(select1, src1[...]).astype(BF16)
            held = ext1
            pltpu.make_async_copy(ext1, cache_out, csem).start()
            unsent.append(lambda: pltpu.make_async_copy(ext1, cache_out, csem).wait())
        valid = (self_key // POS == own_r) & (self_key % POS < CACHE + 1 + t)
        keys = held[0 : SLOTS * POS, :d]
        values = held[0 : SLOTS * POS, d:]
        state = (
            layer_in[t].astype(F32)
            + attend(queries[t].astype(F32), keys, values, valid)
            + cross_s[t]
        )
        resid[t] = state
        centered = state - jnp.mean(state, axis=1, keepdims=True)
        variance = jnp.mean(centered * centered, axis=1, keepdims=True)
        gains = gain[...].astype(F32).reshape(1, d)
        normed = centered * lax.rsqrt(variance + 1e-05) * gains
        for j in range(NB):
            hsend[t, j] = normed[:, j * mc : (j + 1) * mc]

        def make(k):
            to = lax.rem(b + k, NB)
            return hsend.at[t, to], hrecv.at[t, b], to

        to_all(t, 2, make, hsend.at[t, pl.ds(0, NB - 1)])
        hrecv[t, b] = hsend[t, b]

    half = mc // 2

    def halves(x):
        n = x.shape[0] // PER
        left = x[:, :half].reshape(n, PER, half)
        right = x[:, half:].reshape(n, PER, half)
        return jnp.concatenate([left, right], axis=1).astype(BF16)

    def whole(x):
        x = x.astype(F32)
        left = x[:, :PER].reshape(slots, half)
        right = x[:, PER:].reshape(slots, half)
        return jnp.concatenate([left, right], axis=1).astype(BF16)

    def dispatch(t):
        arrive(t, 2)
        rows = hrecv[t].reshape(ROWS, mc).astype(BF16)
        psend[t] = halves(dot(pack_p[t], rows))

        def make(s):
            return psend.at[t, s], xb.at[t, b, s], lax.rem(e + s + shift, ne)

        to_all(
            t, 3, lambda i: make(near_place(i)), psend.at[t, pl.ds(0, mid - 1)], "expert", (1, mid)
        )
        to_all(t, 6, make, psend.at[t, pl.ds(0, mid)], "expert", (mid, ne))
        xb[t, b, own_place] = psend[t, own_place]

    low, high = pl.ds(0, ne // 2), pl.ds(ne // 2, ne // 2)
    every = pl.ds(0, ne)
    up_y, down_y = peer_y(1) * 2, peer_y(3) * 2
    far_y = peer_y(2) * 2

    def ag_copy(t, which):
        block, part, to = (
            (b, every, sib),
            (b, low, up_y + c),
            (b, high, down_y + c),
            (b, high, up_y + c),
            (b, low, down_y + c),
            (down_y + c, low, up_y + c),
            (up_y + c, high, down_y + c),
            (down_y + c, every, sib),
            (up_y + c, every, sib),
            (far_y + c, low, sib),
            (far_y + c, high, sib),
        )[which]
        return pltpu.make_async_remote_copy(
            xb.at[t, block, part], xb.at[t, block, part],
            agsend.at[t, which], agrecv.at[t, which], device_id=(to, e), device_id_type=MESH,
        )

    def gather_start(t):
        arrive(t, 3)
        for which in (1, 4):
            ag_copy(t, which).start()
        arrive(t, 6)
        for which in (2, 3, 0):
            ag_copy(t, which).start()
        for which in range(11):
            unsent.append(lambda which=which: ag_copy(t, which).wait_send())

    def gather_relay(t, stage):
        if stage == 0:
            for came, relay in ((1, 5), (2, 6)):
                ag_copy(t, came).wait_recv()
                ag_copy(t, relay).start()
        else:
            for came, pass_on in ((3, 7), (4, 8)):
                ag_copy(t, came).wait_recv()
                ag_copy(t, pass_on).start()

    def up_part(t, block, first):
        x = whole(xb[t, block])
        at = pl.ds(pl.multiple_of(block * mc, mc), mc)
        for k in range(2):
            part = jnp.dot(x, wup[k, at, :], preferred_element_type=F32)
            if first:
                hid[k] = part
            else:
                hid[k] += part

    def gather_compute(t, between):
        up_part(t, b, True)
        ag_copy(t, 0).wait_recv()
        up_part(t, sib, False)
        up_part(t, down_y + c, False)
        up_part(t, up_y + c, False)
        for came, pass_on in ((5, 9), (6, 10)):
            ag_copy(t, came).wait_recv()
            ag_copy(t, pass_on).start()
        between()
        ag_copy(t, 7).wait_recv()
        up_part(t, down_y + 1 - c, False)
        ag_copy(t, 8).wait_recv()
        up_part(t, up_y + 1 - c, False)
        up_part(t, far_y + c, False)
        ag_copy(t, 9).wait_recv()
        ag_copy(t, 10).wait_recv()
        up_part(t, far_y + 1 - c, False)

    def down_part(t, block, acts):
        at = pl.ds(pl.multiple_of(block * mc, mc), mc)
        return jnp.dot(acts[0], wdn[0, :, at], preferred_element_type=F32) + jnp.dot(
            acts[1], wdn[1, :, at], preferred_element_type=F32
        )

    def sib_copy(t, q):
        return pltpu.make_async_remote_copy(
            sib_s.at[t, q], sib_r.at[t, q],
            sibsend.at[t, q], sibrecv.at[t, q], device_id=(sib, e), device_id_type=MESH,
        )

    def y_copy(t, which):
        to = (up_y, down_y, up_y, down_y, up_y, down_y)[which] + c
        return pltpu.make_async_remote_copy(
            ysend.at[t, which], yrecv.at[t, which],
            sibsend.at[t, 4 + which], sibrecv.at[t, 4 + which],
            device_id=(to, e), device_id_type=MESH,
        )

    first, second = slice(0, slots // 2), slice(slots // 2, slots)

    def y_send(t, which, part):
        ysend[t, which] = part.astype(BF16)
        y_copy(t, which).start()

    def scatter_start(t, between):
        for q in range(4):
            unsent.append(lambda q=q: sib_copy(t, q).wait_send())
        for which in range(6):
            unsent.append(lambda which=which: y_copy(t, which).wait_send())
        own = iota((slots, hid.shape[2]), 0) % PER // CAP
        acts = [
            jnp.where(own == k, jnp.maximum(hid[k], 0.0), 0.0).astype(BF16) for k in range(2)
        ]
        def for_sib(q):
            sib_s[t, q] = down_part(t, peer_y(q) * 2 + (1 - c), acts)
            sib_copy(t, q).start()

        for_sib(2)
        for q, after in ((2, 1), (1, 3), (3, 0), (0, None)):
            if after is not None:
                for_sib(after)
            if q == 3:
                between()
            part = down_part(t, peer_y(q) * 2 + c, acts)
            sib_copy(t, q).wait_recv()
            part = part + sib_r[t, q]
            if q == 2:
                y_send(t, 0, part[first])
                y_send(t, 1, part[second])
            elif q == 1:
                y_send(t, 2, part[second])
                sib_r[t, 1, first] = part[first]
            elif q == 3:
                y_send(t, 3, part[first])
                sib_r[t, 3, second] = part[second]
            else:
                sib_r[t, 0] = part

    def scatter_relay(t):
        y_copy(t, 0).wait_recv()
        y_send(t, 4, sib_r[t, 1, first] + yrecv[t, 0].astype(F32))
        y_copy(t, 1).wait_recv()
        y_send(t, 5, sib_r[t, 3, second] + yrecv[t, 1].astype(F32))

    def give_back(t):
        def make(s):
            return rsend.at[t, s], rrecv.at[t, s], lax.rem(e - s - shift + 2 * ne, ne)

        for which in (2, 5):
            y_copy(t, which).wait_recv()
        total = sib_r[t, 0, second] + yrecv[t, 2].astype(F32) + yrecv[t, 5].astype(F32)
        rsend[t, mid:] = halves(total)
        to_all(t, 7, make, rsend.at[t, pl.ds(0, mid)], "expert", (mid, ne))
        for which in (3, 4):
            y_copy(t, which).wait_recv()
        total = sib_r[t, 0, first] + yrecv[t, 3].astype(F32) + yrecv[t, 4].astype(F32)
        rsend[t, :mid] = halves(total)
        to_all(
            t, 4, lambda i: make(near_place(i)), rsend.at[t, pl.ds(0, mid - 1)], "expert", (1, mid)
        )
        rrecv[t, own_place] = rsend[t, own_place]

    def combine(t):
        arrive(t, 7)
        arrive(t, 4)
        came = whole(rrecv[t])
        mixed = jnp.dot(gate_hi[t], came, preferred_element_type=F32) + jnp.dot(
            gate_lo[t], came, preferred_element_type=F32
        )
        fsend[t] = mixed.reshape(NB, SLOTS, mc)

        def make(k):
            to = lax.rem(b + k, NB)
            return fsend.at[t, to], frecv.at[t, b], to

        to_all(t, 5, make, fsend.at[t, pl.ds(0, NB - 1)])
        frecv[t, b] = fsend[t, b]

    def finish(t):
        arrive(t, 5)
        for j in range(NB):
            cols = slice(j * mc, (j + 1) * mc)
            layer_out[t, :, cols] = (resid[t, :, cols] + frecv[t, j]).astype(BF16)

    attention(0)
    cross(1)
    select1 = select(1, takes1, taken1)
    route(0)
    attention(1)
    dispatch(0)
    route(1)
    dispatch(1)
    gather_start(0)
    up_copy.wait()
    gather_relay(0, 0)
    gather_start(1)
    gather_relay(0, 1)
    gather_compute(0, lambda: None)
    down_copy.wait()
    gather_relay(1, 0)
    scatter_start(0, lambda: gather_relay(1, 1))
    gather_compute(1, lambda: scatter_relay(0))
    scatter_start(1, lambda: None)
    give_back(0)
    scatter_relay(1)
    give_back(1)
    combine(0)
    finish(0)
    combine(1)
    for done in unsent:
        done()
    finish(1)


def emit_kernel(layer_in, cache_in, layer_out, cache_out, layer_v, cache_v, came, left):
    parts = 4
    rows = cache_v.shape[0] // parts
    into, out = [], []
    for k in range(parts):
        part = pl.ds(k * rows, rows)
        into.append(pltpu.make_async_copy(cache_in.at[part], cache_v.at[part], came.at[k]))
        out.append(pltpu.make_async_copy(cache_v.at[part], cache_out.at[part], left.at[k]))
    into.append(pltpu.make_async_copy(layer_in, layer_v, came.at[parts]))
    out.append(pltpu.make_async_copy(layer_v, layer_out, left.at[parts]))
    for copy in into:
        copy.start()
    for first, then in zip(into, out):
        first.wait()
        then.start()
    for copy in out:
        copy.wait()


def shards(
    layer_in, queries, fresh_entries, cross_queries, past_cache, encoder_states, source_lengths,
    parents, expert_ids, gate_weights, norm_gain, up_weight, down_weight,
):
    ne = lax.axis_size("expert")
    d = HEADS * DH
    mc = d // NB
    half = mc // 2
    kc = 2 * d // NB
    slots = ne * PER
    hs = up_weight.shape[2]
    vmem = pl.BlockSpec(memory_space=pltpu.VMEM)
    smem = pl.BlockSpec(memory_space=pltpu.SMEM)
    hbm = pl.BlockSpec(memory_space=pl.ANY)
    dma = pltpu.SemaphoreType.DMA
    layer_out, cache_out = pl.pallas_call(
        functools.partial(layer_kernel, ne),
        out_shape=(
            jax.ShapeDtypeStruct((STEPS, SLOTS, d), BF16),
            jax.ShapeDtypeStruct((SLOTS * POS, 2 * d), BF16),
        ),
        in_specs=[smem] + [vmem] * 4 + [hbm] * 8,
        out_specs=(vmem, hbm),
        scratch_shapes=[
            pltpu.VMEM((CACHE, SLOTS, 2 * d), BF16),
            pltpu.VMEM((STEPS, SLOTS, 2 * d), BF16),
            pltpu.VMEM((STEPS, SLOTS, d), BF16),
            pltpu.VMEM((2, 32, 2 * d), BF16),
            pltpu.VMEM((STEPS, SLOTS, d), BF16),
            pltpu.VMEM((STEPS, SLOTS, d), BF16),
            pltpu.VMEM((2, d, hs), BF16),
            pltpu.VMEM((2, hs, d), BF16),
            pltpu.VMEM((CACHE * SLOTS + 2 * POS + POS, 2 * d), BF16),
            pltpu.VMEM((SLOTS * POS + 2 * POS + POS, 2 * d), BF16),
            pltpu.VMEM((SLOTS * POS, 2 * d), BF16),
            pltpu.VMEM((STEPS, 2 * POS, 2 * d), BF16),
            pltpu.VMEM((2 * NB * POS, kc), BF16),
            pltpu.VMEM((2 * NB * POS, kc), BF16),
            pltpu.VMEM((STEPS, 2 * NB * POS, kc), BF16),
            pltpu.VMEM((STEPS, SLOTS, d), F32),
            pltpu.VMEM((STEPS, SLOTS, d), F32),
            pltpu.VMEM((STEPS, slots, ROWS), BF16),
            pltpu.VMEM((STEPS, ROWS, slots), BF16),
            pltpu.VMEM((STEPS, ROWS, slots), BF16),
            pltpu.VMEM((STEPS, NB, SLOTS, mc), F32),
            pltpu.VMEM((STEPS, NB, SLOTS, mc), F32),
            pltpu.VMEM((STEPS, ne, 2 * PER, half), BF16),
            pltpu.VMEM((STEPS, NB, ne, 2 * PER, half), BF16),
            pltpu.VMEM((2, slots, hs), F32),
            pltpu.VMEM((STEPS, 4, slots, mc), F32),
            pltpu.VMEM((STEPS, 4, slots, mc), F32),
            pltpu.VMEM((STEPS, 6, slots // 2, mc), BF16),
            pltpu.VMEM((STEPS, 6, slots // 2, mc), BF16),
            pltpu.VMEM((STEPS, ne, 2 * PER, half), BF16),
            pltpu.VMEM((STEPS, ne, 2 * PER, half), BF16),
            pltpu.VMEM((STEPS, NB, SLOTS, mc), F32),
            pltpu.VMEM((STEPS, NB, SLOTS, mc), F32),
            dma((6,)),
            dma((2,)),
            dma((STEPS, 2)),
            dma,
            dma((STEPS, 8)),
            dma((STEPS, 8)),
            dma((STEPS, 11)),
            dma((STEPS, 11)),
            dma((STEPS, 10)),
            dma((STEPS, 10)),
        ],
        compiler_params=pltpu.CompilerParams(
            collective_id=1, has_side_effects=True, vmem_limit_bytes=56 * 2**20
        ),
        cost_estimate=pl.CostEstimate(
            flops=4 * STEPS * slots * d * hs * 2, bytes_accessed=12 * 2**20, transcendentals=0
        ),
        name="layer",
    )(
        source_lengths, parents[:, 0], jnp.transpose(expert_ids[:, 0], (0, 2, 1)),
        jnp.transpose(gate_weights[:, 0], (0, 2, 1)), norm_gain,
        jnp.transpose(past_cache[0], (1, 0, 2)), fresh_entries[:, 0], cross_queries[:, 0],
        encoder_states[0], queries[:, 0], layer_in[:, 0], up_weight, down_weight,
    )
    layer_out, cache_out = pl.pallas_call(
        emit_kernel,
        out_shape=(
            jax.ShapeDtypeStruct((STEPS, SLOTS, d), BF16),
            jax.ShapeDtypeStruct((SLOTS * POS, 2 * d), BF16),
        ),
        in_specs=[hbm, hbm],
        out_specs=(hbm, hbm),
        scratch_shapes=[
            pltpu.VMEM((STEPS, SLOTS, d), BF16),
            pltpu.VMEM((SLOTS * POS, 2 * d), BF16),
            dma((5,)),
            dma((5,)),
        ],
        name="emit",
    )(layer_out, cache_out)
    return layer_out[:, None], cache_out.reshape(1, SLOTS, POS, 2 * d)


def solution(mesh):
    in_specs = (
        P(None, "expert", "batch", None),
        P(None, "expert", "batch", None),
        P(None, "expert", "batch", None),
        P(None, "expert", "batch", None),
        P("expert", "batch", None, None),
        P("expert", "batch", None, None),
        P("expert", "batch"),
        P(None, "expert", None),
        P(None, "expert", None, None),
        P(None, "expert", None, None),
        P(),
        P("expert", None, "batch"),
        P("expert", "batch", None),
    )
    out_specs = (P(None, "expert", "batch", None), P("expert", "batch", None, None))
    return jax.shard_map(shards, mesh=mesh, in_specs=in_specs, out_specs=out_specs, check_vma=False)
```

```python
import functools

import jax
import jax.numpy as jnp
from jax import lax
from jax.experimental import pallas as pl
from jax.experimental.pallas import tpu as pltpu
from jax.sharding import PartitionSpec as P

HEADS = 16
DH = 128
CAP = 4
STEPS = 2
SLOTS = 8
BEAM = 4
CACHE = 14
NB = 8
ROWS = NB * SLOTS
PER = 2 * CAP
POS = 16
MESH = pl.DeviceIdType.MESH
F32 = jnp.float32
BF16 = jnp.bfloat16


def iota(shape, dim):
    return lax.broadcasted_iota(jnp.int32, shape, dim)


def hot(mask):
    return jnp.where(mask, 1.0, 0.0).astype(BF16)


def dot(x, y):
    return jnp.dot(x, y, preferred_element_type=F32)


def move_plan(par):
    n = ROWS
    row, col = iota((n, n), 1), iota((n, n), 0)
    dev_r, dev_c = row // SLOTS, col // SLOTS
    before = jnp.where((row < col) & (dev_r == dev_c), 1.0, 0.0)

    def across(x):
        return jnp.broadcast_to(jnp.sum(x, axis=1, keepdims=True), (n, n))

    def down(x):
        return jnp.broadcast_to(jnp.sum(x, axis=0, keepdims=True), (n, n))

    eye = jnp.where(row == col, 1.0, 0.0)
    par_r = jnp.broadcast_to(par, (n, n))
    takes = jnp.where(col == par_r, 1.0, 0.0)
    cross_r = jnp.where(par_r // SLOTS != dev_r, 1.0, 0.0)
    cross_c = across(eye * cross_r)
    leave_c = across(takes * cross_r)
    leave_r = down(eye * leave_c)
    give_c = across(before * leave_r) + 2.0 * dev_c.astype(F32)
    give_r = down(eye * give_c)
    take_c = across(before * cross_r) + 2.0 * dev_c.astype(F32)
    take_r = down(eye * take_c)
    rowf, colf = row.astype(F32), col.astype(F32)
    given = jnp.where(rowf == give_c, leave_c, 0.0).astype(BF16)
    given_t = jnp.where(colf == give_r, leave_r, 0.0).astype(BF16)
    taken = jnp.where(rowf == take_c, cross_c, 0.0).astype(BF16)
    taken_t = jnp.where(colf == take_r, cross_r, 0.0).astype(BF16)
    takes_t = jnp.transpose(takes).astype(BF16)
    return takes_t, given, given_t, taken, taken_t


def head_mask(rows):
    head = iota((rows, HEADS, HEADS * DH), 1)
    column = iota((rows, HEADS, HEADS * DH), 2) // DH
    return (head == column).astype(F32)


def attend(q, keys, values, valid):
    d = HEADS * DH
    mask = head_mask(SLOTS)
    spread = (jnp.broadcast_to(q[:, None, :], (SLOTS, HEADS, d)) * mask).reshape(SLOTS * HEADS, d)
    scores = lax.dot_general(
        spread.astype(BF16), keys, (((1,), (1,)), ((), ())), preferred_element_type=F32
    ) * (1.0 / DH**0.5)
    scores = jnp.where(valid, scores, -1e30)
    raised = jnp.where(valid, jnp.exp(scores - jnp.max(scores, axis=1, keepdims=True)), 0.0)
    weights = (raised / jnp.sum(raised, axis=1, keepdims=True)).astype(BF16)
    out = jnp.dot(weights, values, preferred_element_type=F32)
    return jnp.sum(out.reshape(SLOTS, HEADS, d) * mask, axis=1)


def layer_kernel(
    ne,
    lens, par, ids, gates, gain, cache_h, fresh_h, cross_h, enc_h, queries_h, layer_h, up_hbm, down_hbm,
    layer_out, cache_out,
    cache, fresh, cross_q, enc, queries, layer_in, wup, wdn, src0, src1, ext1, st_a, pool0, pool1, st_b, cross_s, resid,
    pack_p, gate_hi, gate_lo, hsend, hrecv, psend, xb, hid, sib_s, sib_r, ysend, yrecv,
    rsend, rrecv, fsend, frecv, osem, wsem, lsem, csem, bsend, brecv, agsend, agrecv, sibsend, sibrecv,
):
    b, e = lax.axis_index("batch"), lax.axis_index("expert")
    y, c = b // 2, b % 2
    sib = y * 2 + (1 - c)
    d = HEADS * DH
    kc = 2 * d // NB
    mc = d // NB
    slots = ne * PER
    unsent, unreceived = [], {}
    operands = [
        pltpu.make_async_copy(src, dst, osem.at[k])
        for k, (src, dst) in enumerate(
            (
                (cache_h, cache),
                (fresh_h, fresh),
                (cross_h, cross_q),
                (enc_h, enc),
                (queries_h, queries),
                (layer_h, layer_in),
            )
        )
    ]
    for copy in operands:
        copy.start()

    def peer_y(q):
        return lax.rem(y + q, 4)

    barrier = pltpu.get_barrier_semaphore()

    def greet_b(k, _):
        pl.semaphore_signal(
            barrier, inc=1, device_id=(lax.rem(b + k, NB), e), device_id_type=MESH
        )
        return 0

    def greet_e(k, _):
        pl.semaphore_signal(
            barrier, inc=1, device_id=(b, lax.rem(e + k, ne)), device_id_type=MESH
        )
        return 0

    lax.fori_loop(1, NB, greet_b, 0, unroll=True)
    lax.fori_loop(1, ne, greet_e, 0, unroll=True)

    up_copy = pltpu.make_async_copy(up_hbm, wup, wsem.at[0])
    down_copy = pltpu.make_async_copy(down_hbm, wdn, wsem.at[1])

    def local(t, phase, src, dst):
        copy = pltpu.make_async_copy(src, dst, lsem.at[t, phase])
        copy.start()
        others = unreceived[t, phase]

        def both():
            others()
            copy.wait()

        unreceived[t, phase] = both

    def wait_bytes(ref, sem):
        pltpu.make_async_copy(ref, ref, sem).wait()

    def to_all(t, phase, make, ref, axis="batch", span=(1, NB)):
        if span[0] == span[1]:
            unreceived[t, phase] = lambda: None
            return

        def one(k, _):
            src, dst, to = make(k)
            to = (to, e) if axis == "batch" else (b, to)
            pltpu.make_async_remote_copy(
                src, dst, bsend.at[t, phase], brecv.at[t, phase], device_id=to, device_id_type=MESH
            ).start()
            return 0

        lax.fori_loop(span[0], span[1], one, 0, unroll=True)
        unsent.append(lambda: wait_bytes(ref, bsend.at[t, phase]))
        unreceived[t, phase] = lambda: wait_bytes(ref, brecv.at[t, phase])

    mid = ne // 2
    shift = 3 * ne // 4 if ne % 4 == 0 else 0
    own_place = (ne - shift) % ne

    def near_place(i):
        return lax.rem(own_place + i, mid)

    def arrive(t, phase):
        unreceived.pop((t, phase))()

    takes0, given0, given0_t, taken0, taken0_t = move_plan(par[0:1, :])

    near, late = CACHE * SLOTS, CACHE * SLOTS + 2 * POS
    operands[0].wait()
    src0[0:near] = cache[...].astype(F32).reshape(near, 2 * d).astype(BF16)

    same_dev = iota((ROWS, ROWS), 0) // SLOTS == iota((ROWS, ROWS), 1) // SLOTS
    own_m = hot(iota((2 * POS, ROWS), 1) == 2 * b + iota((2 * POS, ROWS), 0) // POS)
    near_c = hot(iota((ROWS, near), 0) == SLOTS * b + iota((ROWS, near), 1) % SLOTS)
    near_p = iota((2 * POS, near), 0) % POS == iota((2 * POS, near), 1) // SLOTS

    def given_rows(chosen):
        pick = dot(dot(own_m, chosen).astype(BF16), near_c)
        return dot(jnp.where(near_p, pick, 0.0).astype(BF16), src0[0:near])

    st_a[0] = given_rows(given0_t).astype(BF16)

    pl.semaphore_wait(barrier, NB - 1 + ne - 1)

    pools = (pool0, pool1)

    def own_cols(k):
        return pl.ds(pl.multiple_of(k * kc, kc), kc)

    def own_rows(k):
        return pl.ds(pl.multiple_of(k * 2 * POS, 2 * POS), 2 * POS)

    def send_a(t):
        def make(k):
            to = lax.rem(b + k, NB)
            return st_a.at[t, :, own_cols(to)], pools[t].at[own_rows(b)], to

        to_all(t, 0, make, st_b.at[t, pl.ds(0, 14 * POS)])
        local(t, 0, st_a.at[t, :, own_cols(b)], pools[t].at[own_rows(b)])

    def send_b(t):
        landing = src0.at[near:late] if t == 0 else src1.at[SLOTS * POS : SLOTS * POS + 2 * POS]

        def make(k):
            to = lax.rem(b + k, NB)
            return st_b.at[t, own_rows(to)], landing.at[:, own_cols(b)], to

        to_all(t, 1, make, st_b.at[t, pl.ds(0, 14 * POS)])
        local(t, 1, st_b.at[t, own_rows(b)], landing.at[:, own_cols(b)])

    send_a(0)
    up_copy.start()
    down_copy.start()
    operands[1].wait()
    blank = jnp.zeros((SLOTS, 2 * d), F32)
    src0[late:] = jnp.concatenate([fresh[0].astype(F32), blank], axis=0).astype(BF16)
    src1[late + POS :] = jnp.concatenate([fresh[1].astype(F32), blank], axis=0).astype(BF16)

    takes1, given1, given1_t, taken1, taken1_t = move_plan(par[1:2, :])
    kept1_t = dot(given1_t, jnp.where(same_dev, takes0.astype(F32), 0.0).astype(BF16)).astype(BF16)
    slot_c = hot(
        (iota((ROWS, POS), 0) == SLOTS * b + iota((ROWS, POS), 1)) & (iota((ROWS, POS), 1) < SLOTS)
    )
    entry = dot(dot(own_m, given1_t).astype(BF16), slot_c)
    entry = jnp.where(iota((2 * POS, POS), 0) % POS == CACHE, entry, 0.0).astype(BF16)
    st_a[1] = (given_rows(kept1_t) + dot(entry, src0[late:])).astype(BF16)
    send_a(1)

    own_s = iota((SLOTS * HEADS, 64), 0) // (HEADS * BEAM)
    key_i = iota((SLOTS * HEADS, 64), 1)
    limit = jnp.where(own_s == 0, lens[0, 0], lens[0, 1])
    cross_valid = (key_i // 32 == own_s) & (key_i % 32 < limit)

    def cross(t):
        enc_k = enc[:, :, :d].reshape(64, d)
        enc_v = enc[:, :, d:].reshape(64, d)
        cross_s[t] = attend(cross_q[t].astype(F32), enc_k, enc_v, cross_valid)

    def route(t):
        slot = iota((slots, ROWS), 0)
        owner = lax.rem(slot // PER + shift + e, ne)
        expert = owner * 2 + slot % PER // CAP
        earlier = hot(iota((ROWS, ROWS), 0) < iota((ROWS, ROWS), 1))
        first = jnp.where(ids[t, 0:1, :] == expert, 1.0, 0.0)
        second = jnp.where(ids[t, 1:2, :] == expert, 1.0, 0.0)
        named = first + second
        rank = dot(named.astype(BF16), earlier)
        chosen = jnp.where(rank == (slot % CAP).astype(F32), named, 0.0)
        pack_p[t] = chosen.astype(BF16)
        weight = chosen * (first * gates[t, 0:1, :] + second * gates[t, 1:2, :])
        weight = jnp.transpose(weight)
        high = weight.astype(BF16)
        gate_hi[t] = high
        gate_lo[t] = (weight - high.astype(F32)).astype(BF16)

    pairs = 2 * NB * POS
    pair_m = hot(iota((pairs, ROWS), 0) // POS == iota((pairs, ROWS), 1))
    pair_mt = hot(iota((ROWS, pairs), 0) == iota((ROWS, pairs), 1) // POS)
    same_p = iota((pairs, pairs), 0) % POS == iota((pairs, pairs), 1) % POS

    def spread(small):
        wide = dot(dot(pair_m, small.astype(BF16)).astype(BF16), pair_mt)
        return jnp.where(same_p, wide, 0.0).astype(BF16)

    from0 = dot(takes0, given0).astype(BF16)
    hand0 = spread(dot(taken0_t, from0))

    def select(t, takes, taken):
        held = near if t == 0 else SLOTS * POS
        width = held + 2 * POS + POS
        shape = (SLOTS * POS, width)
        k, out_p, out_r = iota(shape, 1), iota(shape, 0) % POS, iota(shape, 0) // POS
        own_r = hot(
            iota((SLOTS * POS, ROWS), 1) == SLOTS * b + iota((SLOTS * POS, ROWS), 0) // POS
        )
        kk, cc = iota((ROWS, width), 1), iota((ROWS, width), 0)
        slot = kk % SLOTS if t == 0 else kk // POS
        at_c = hot((kk < held) & (cc == SLOTS * b + slot))
        at_m = hot((kk >= held) & (kk < held + 2 * POS) & (cc == 2 * b + (kk - held) // POS))
        picked = dot(dot(own_r, takes).astype(BF16), at_c)
        picked = picked + dot(dot(own_r, taken).astype(BF16), at_m)
        old_p = k // SLOTS if t == 0 else k % POS
        key_p = jnp.where(k < held, old_p, (k - held) % POS)
        picked = jnp.where((key_p == out_p) & (k < held + 2 * POS), picked, 0.0)
        new = (k - (held + 2 * POS) == out_r) & (out_p == CACHE + t)
        return jnp.where(new, 1.0, picked).astype(BF16)

    via1 = dot(taken1_t, takes1).astype(BF16)
    arrive(0, 0)
    st_b[0] = dot(hand0, pool0[...]).astype(BF16)
    send_b(0)
    hand1_old = spread(dot(via1, from0))
    hand1_new = spread(dot(via1, given1))
    select0 = select(0, takes0, taken0)
    for copy in operands[2:]:
        copy.wait()
    cross(0)
    arrive(1, 0)
    st_b[1] = (dot(hand1_old, pool0[...]) + dot(hand1_new, pool1[...])).astype(BF16)
    send_b(1)

    own_r = iota((SLOTS * HEADS, SLOTS * POS), 0) // HEADS
    self_key = iota((SLOTS * HEADS, SLOTS * POS), 1)

    def attention(t):
        arrive(t, 1)
        if t == 0:
            src1[0 : SLOTS * POS] = dot(select0, src0[...]).astype(BF16)
            held = src1
        else:
            ext1[...] = dot(select1, src1[...]).astype(BF16)
            held = ext1
            pltpu.make_async_copy(ext1, cache_out, csem).start()
            unsent.append(lambda: pltpu.make_async_copy(ext1, cache_out, csem).wait())
        valid = (self_key // POS == own_r) & (self_key % POS < CACHE + 1 + t)
        keys = held[0 : SLOTS * POS, :d]
        values = held[0 : SLOTS * POS, d:]
        state = (
            layer_in[t].astype(F32)
            + attend(queries[t].astype(F32), keys, values, valid)
            + cross_s[t]
        )
        resid[t] = state
        centered = state - jnp.mean(state, axis=1, keepdims=True)
        variance = jnp.mean(centered * centered, axis=1, keepdims=True)
        gains = gain[...].astype(F32).reshape(1, d)
        normed = centered * lax.rsqrt(variance + 1e-05) * gains
        for j in range(NB):
            hsend[t, j] = normed[:, j * mc : (j + 1) * mc]

        def make(k):
            to = lax.rem(b + k, NB)
            return hsend.at[t, to], hrecv.at[t, b], to

        to_all(t, 2, make, hsend.at[t, pl.ds(0, NB - 1)])
        hrecv[t, b] = hsend[t, b]

    half = mc // 2

    def halves(x):
        n = x.shape[0] // PER
        left = x[:, :half].reshape(n, PER, half)
        right = x[:, half:].reshape(n, PER, half)
        return jnp.concatenate([left, right], axis=1).astype(BF16)

    def whole(x):
        x = x.astype(F32)
        left = x[:, :PER].reshape(slots, half)
        right = x[:, PER:].reshape(slots, half)
        return jnp.concatenate([left, right], axis=1).astype(BF16)

    def dispatch(t):
        arrive(t, 2)
        rows = hrecv[t].reshape(ROWS, mc).astype(BF16)
        psend[t] = halves(dot(pack_p[t], rows))

        def make(s):
            return psend.at[t, s], xb.at[t, b, s], lax.rem(e + s + shift, ne)

        to_all(
            t, 3, lambda i: make(near_place(i)), psend.at[t, pl.ds(0, mid - 1)], "expert", (1, mid)
        )
        to_all(t, 6, make, psend.at[t, pl.ds(0, mid)], "expert", (mid, ne))
        xb[t, b, own_place] = psend[t, own_place]

    low, high = pl.ds(0, ne // 2), pl.ds(ne // 2, ne // 2)
    every = pl.ds(0, ne)
    up_y, down_y = peer_y(1) * 2, peer_y(3) * 2
    far_y = peer_y(2) * 2

    def ag_copy(t, which):
        block, part, to = (
            (b, every, sib),
            (b, low, up_y + c),
            (b, high, down_y + c),
            (b, high, up_y + c),
            (b, low, down_y + c),
            (down_y + c, low, up_y + c),
            (up_y + c, high, down_y + c),
            (down_y + c, every, sib),
            (up_y + c, every, sib),
            (far_y + c, low, sib),
            (far_y + c, high, sib),
        )[which]
        return pltpu.make_async_remote_copy(
            xb.at[t, block, part], xb.at[t, block, part],
            agsend.at[t, which], agrecv.at[t, which], device_id=(to, e), device_id_type=MESH,
        )

    def gather_start(t):
        arrive(t, 3)
        for which in (1, 4):
            ag_copy(t, which).start()
        arrive(t, 6)
        for which in (2, 3, 0):
            ag_copy(t, which).start()
        for which in range(11):
            unsent.append(lambda which=which: ag_copy(t, which).wait_send())

    def gather_relay(t, stage):
        if stage == 0:
            for came, relay in ((1, 5), (2, 6)):
                ag_copy(t, came).wait_recv()
                ag_copy(t, relay).start()
        else:
            for came, pass_on in ((3, 7), (4, 8)):
                ag_copy(t, came).wait_recv()
                ag_copy(t, pass_on).start()

    def up_part(t, block, first):
        x = whole(xb[t, block])
        at = pl.ds(pl.multiple_of(block * mc, mc), mc)
        for k in range(2):
            part = jnp.dot(x, wup[k, at, :], preferred_element_type=F32)
            if first:
                hid[k] = part
            else:
                hid[k] += part

    def gather_compute(t, between):
        up_part(t, b, True)
        ag_copy(t, 0).wait_recv()
        up_part(t, sib, False)
        up_part(t, down_y + c, False)
        up_part(t, up_y + c, False)
        for came, pass_on in ((5, 9), (6, 10)):
            ag_copy(t, came).wait_recv()
            ag_copy(t, pass_on).start()
        between()
        ag_copy(t, 7).wait_recv()
        up_part(t, down_y + 1 - c, False)
        ag_copy(t, 8).wait_recv()
        up_part(t, up_y + 1 - c, False)
        up_part(t, far_y + c, False)
        ag_copy(t, 9).wait_recv()
        ag_copy(t, 10).wait_recv()
        up_part(t, far_y + 1 - c, False)

    def down_part(t, block, acts):
        at = pl.ds(pl.multiple_of(block * mc, mc), mc)
        return jnp.dot(acts[0], wdn[0, :, at], preferred_element_type=F32) + jnp.dot(
            acts[1], wdn[1, :, at], preferred_element_type=F32
        )

    def sib_copy(t, q):
        return pltpu.make_async_remote_copy(
            sib_s.at[t, q], sib_r.at[t, q],
            sibsend.at[t, q], sibrecv.at[t, q], device_id=(sib, e), device_id_type=MESH,
        )

    def y_copy(t, which):
        to = (up_y, down_y, up_y, down_y, up_y, down_y)[which] + c
        return pltpu.make_async_remote_copy(
            ysend.at[t, which], yrecv.at[t, which],
            sibsend.at[t, 4 + which], sibrecv.at[t, 4 + which],
            device_id=(to, e), device_id_type=MESH,
        )

    first, second = slice(0, slots // 2), slice(slots // 2, slots)

    def y_send(t, which, part):
        ysend[t, which] = part.astype(BF16)
        y_copy(t, which).start()

    def scatter_start(t, between):
        for q in range(4):
            unsent.append(lambda q=q: sib_copy(t, q).wait_send())
        for which in range(6):
            unsent.append(lambda which=which: y_copy(t, which).wait_send())
        own = iota((slots, hid.shape[2]), 0) % PER // CAP
        acts = [
            jnp.where(own == k, jnp.maximum(hid[k], 0.0), 0.0).astype(BF16) for k in range(2)
        ]
        def for_sib(q):
            sib_s[t, q] = down_part(t, peer_y(q) * 2 + (1 - c), acts)
            sib_copy(t, q).start()

        for_sib(2)
        for q, after in ((2, 1), (1, 3), (3, 0), (0, None)):
            if after is not None:
                for_sib(after)
            if q == 3:
                between()
            part = down_part(t, peer_y(q) * 2 + c, acts)
            sib_copy(t, q).wait_recv()
            part = part + sib_r[t, q]
            if q == 2:
                y_send(t, 0, part[first])
                y_send(t, 1, part[second])
            elif q == 1:
                y_send(t, 2, part[second])
                sib_r[t, 1, first] = part[first]
            elif q == 3:
                y_send(t, 3, part[first])
                sib_r[t, 3, second] = part[second]
            else:
                sib_r[t, 0] = part

    def scatter_relay(t):
        y_copy(t, 0).wait_recv()
        y_send(t, 4, sib_r[t, 1, first] + yrecv[t, 0].astype(F32))
        y_copy(t, 1).wait_recv()
        y_send(t, 5, sib_r[t, 3, second] + yrecv[t, 1].astype(F32))

    def give_back(t):
        def make(s):
            return rsend.at[t, s], rrecv.at[t, s], lax.rem(e - s - shift + 2 * ne, ne)

        for which in (2, 5):
            y_copy(t, which).wait_recv()
        total = sib_r[t, 0, second] + yrecv[t, 2].astype(F32) + yrecv[t, 5].astype(F32)
        rsend[t, mid:] = halves(total)
        to_all(t, 7, make, rsend.at[t, pl.ds(0, mid)], "expert", (mid, ne))
        for which in (3, 4):
            y_copy(t, which).wait_recv()
        total = sib_r[t, 0, first] + yrecv[t, 3].astype(F32) + yrecv[t, 4].astype(F32)
        rsend[t, :mid] = halves(total)
        to_all(
            t, 4, lambda i: make(near_place(i)), rsend.at[t, pl.ds(0, mid - 1)], "expert", (1, mid)
        )
        rrecv[t, own_place] = rsend[t, own_place]

    def combine(t):
        arrive(t, 7)
        arrive(t, 4)
        came = whole(rrecv[t])
        mixed = jnp.dot(gate_hi[t], came, preferred_element_type=F32) + jnp.dot(
            gate_lo[t], came, preferred_element_type=F32
        )
        fsend[t] = mixed.reshape(NB, SLOTS, mc)

        def make(k):
            to = lax.rem(b + k, NB)
            return fsend.at[t, to], frecv.at[t, b], to

        to_all(t, 5, make, fsend.at[t, pl.ds(0, NB - 1)])
        frecv[t, b] = fsend[t, b]

    def finish(t):
        arrive(t, 5)
        for j in range(NB):
            cols = slice(j * mc, (j + 1) * mc)
            layer_out[t, :, cols] = (resid[t, :, cols] + frecv[t, j]).astype(BF16)

    attention(0)
    cross(1)
    select1 = select(1, takes1, taken1)
    route(0)
    attention(1)
    dispatch(0)
    route(1)
    dispatch(1)
    gather_start(0)
    up_copy.wait()
    gather_relay(0, 0)
    gather_start(1)
    gather_relay(0, 1)
    gather_compute(0, lambda: None)
    down_copy.wait()
    gather_relay(1, 0)
    scatter_start(0, lambda: gather_relay(1, 1))
    gather_compute(1, lambda: scatter_relay(0))
    scatter_start(1, lambda: None)
    give_back(0)
    scatter_relay(1)
    give_back(1)
    combine(0)
    finish(0)
    combine(1)
    for done in unsent:
        done()
    finish(1)


def emit_kernel(layer_in, cache_in, layer_out, cache_out, layer_v, cache_v, came, left):
    parts = 4
    rows = cache_v.shape[0] // parts
    into, out = [], []
    for k in range(parts):
        part = pl.ds(k * rows, rows)
        into.append(pltpu.make_async_copy(cache_in.at[part], cache_v.at[part], came.at[k]))
        out.append(pltpu.make_async_copy(cache_v.at[part], cache_out.at[part], left.at[k]))
    into.append(pltpu.make_async_copy(layer_in, layer_v, came.at[parts]))
    out.append(pltpu.make_async_copy(layer_v, layer_out, left.at[parts]))
    for copy in into:
        copy.start()
    for first, then in zip(into, out):
        first.wait()
        then.start()
    for copy in out:
        copy.wait()


def shards(
    layer_in, queries, fresh_entries, cross_queries, past_cache, encoder_states, source_lengths,
    parents, expert_ids, gate_weights, norm_gain, up_weight, down_weight,
):
    ne = lax.axis_size("expert")
    d = HEADS * DH
    mc = d // NB
    half = mc // 2
    kc = 2 * d // NB
    slots = ne * PER
    hs = up_weight.shape[2]
    vmem = pl.BlockSpec(memory_space=pltpu.VMEM)
    smem = pl.BlockSpec(memory_space=pltpu.SMEM)
    hbm = pl.BlockSpec(memory_space=pl.ANY)
    dma = pltpu.SemaphoreType.DMA
    layer_out, cache_out = pl.pallas_call(
        functools.partial(layer_kernel, ne),
        out_shape=(
            jax.ShapeDtypeStruct((STEPS, SLOTS, d), BF16),
            jax.ShapeDtypeStruct((SLOTS * POS, 2 * d), BF16),
        ),
        in_specs=[smem] + [vmem] * 4 + [hbm] * 8,
        out_specs=(vmem, hbm),
        scratch_shapes=[
            pltpu.VMEM((CACHE, SLOTS, 2 * d), BF16),
            pltpu.VMEM((STEPS, SLOTS, 2 * d), BF16),
            pltpu.VMEM((STEPS, SLOTS, d), BF16),
            pltpu.VMEM((2, 32, 2 * d), BF16),
            pltpu.VMEM((STEPS, SLOTS, d), BF16),
            pltpu.VMEM((STEPS, SLOTS, d), BF16),
            pltpu.VMEM((2, d, hs), BF16),
            pltpu.VMEM((2, hs, d), BF16),
            pltpu.VMEM((CACHE * SLOTS + 2 * POS + POS, 2 * d), BF16),
            pltpu.VMEM((SLOTS * POS + 2 * POS + POS, 2 * d), BF16),
            pltpu.VMEM((SLOTS * POS, 2 * d), BF16),
            pltpu.VMEM((STEPS, 2 * POS, 2 * d), BF16),
            pltpu.VMEM((2 * NB * POS, kc), BF16),
            pltpu.VMEM((2 * NB * POS, kc), BF16),
            pltpu.VMEM((STEPS, 2 * NB * POS, kc), BF16),
            pltpu.VMEM((STEPS, SLOTS, d), F32),
            pltpu.VMEM((STEPS, SLOTS, d), F32),
            pltpu.VMEM((STEPS, slots, ROWS), BF16),
            pltpu.VMEM((STEPS, ROWS, slots), BF16),
            pltpu.VMEM((STEPS, ROWS, slots), BF16),
            pltpu.VMEM((STEPS, NB, SLOTS, mc), F32),
            pltpu.VMEM((STEPS, NB, SLOTS, mc), F32),
            pltpu.VMEM((STEPS, ne, 2 * PER, half), BF16),
            pltpu.VMEM((STEPS, NB, ne, 2 * PER, half), BF16),
            pltpu.VMEM((2, slots, hs), F32),
            pltpu.VMEM((STEPS, 4, slots, mc), F32),
            pltpu.VMEM((STEPS, 4, slots, mc), F32),
            pltpu.VMEM((STEPS, 6, slots // 2, mc), BF16),
            pltpu.VMEM((STEPS, 6, slots // 2, mc), BF16),
            pltpu.VMEM((STEPS, ne, 2 * PER, half), BF16),
            pltpu.VMEM((STEPS, ne, 2 * PER, half), BF16),
            pltpu.VMEM((STEPS, NB, SLOTS, mc), F32),
            pltpu.VMEM((STEPS, NB, SLOTS, mc), F32),
            dma((6,)),
            dma((2,)),
            dma((STEPS, 2)),
            dma,
            dma((STEPS, 8)),
            dma((STEPS, 8)),
            dma((STEPS, 11)),
            dma((STEPS, 11)),
            dma((STEPS, 10)),
            dma((STEPS, 10)),
        ],
        compiler_params=pltpu.CompilerParams(
            collective_id=1, has_side_effects=True, vmem_limit_bytes=56 * 2**20
        ),
        cost_estimate=pl.CostEstimate(
            flops=4 * STEPS * slots * d * hs * 2, bytes_accessed=12 * 2**20, transcendentals=0
        ),
        name="layer",
    )(
        source_lengths, parents[:, 0], jnp.transpose(expert_ids[:, 0], (0, 2, 1)),
        jnp.transpose(gate_weights[:, 0], (0, 2, 1)), norm_gain,
        jnp.transpose(past_cache[0], (1, 0, 2)), fresh_entries[:, 0], cross_queries[:, 0],
        encoder_states[0], queries[:, 0], layer_in[:, 0], up_weight, down_weight,
    )
    layer_out, cache_out = pl.pallas_call(
        emit_kernel,
        out_shape=(
            jax.ShapeDtypeStruct((STEPS, SLOTS, d), BF16),
            jax.ShapeDtypeStruct((SLOTS * POS, 2 * d), BF16),
        ),
        in_specs=[hbm, hbm],
        out_specs=(hbm, hbm),
        scratch_shapes=[
            pltpu.VMEM((STEPS, SLOTS, d), BF16),
            pltpu.VMEM((SLOTS * POS, 2 * d), BF16),
            dma((5,)),
            dma((5,)),
        ],
        name="emit",
    )(layer_out, cache_out)
    return layer_out[:, None], cache_out.reshape(1, SLOTS, POS, 2 * d)


def solution(mesh):
    in_specs = (
        P(None, "expert", "batch", None),
        P(None, "expert", "batch", None),
        P(None, "expert", "batch", None),
        P(None, "expert", "batch", None),
        P("expert", "batch", None, None),
        P("expert", "batch", None, None),
        P("expert", "batch"),
        P(None, "expert", None),
        P(None, "expert", None, None),
        P(None, "expert", None, None),
        P(),
        P("expert", None, "batch"),
        P("expert", "batch", None),
    )
    out_specs = (P(None, "expert", "batch", None), P("expert", "batch", None, None))
    return jax.shard_map(shards, mesh=mesh, in_specs=in_specs, out_specs=out_specs, check_vma=False)
```
